32 devices in a mesh: space: 4 (over x, core), code: 4 (over z), clip: 2 (over y).
Axes of the slice: x: 2, y: 2, z: 4, core: 2. Of those that a mesh axis runs over, the one named last changes fastest.
Arguments:
- soft_weights: bfloat16 [2, 256, 32, 8192], P('clip', 'space', None, 'code'), may hold values from 0.00029945374 to 0.029907227
- codebook: bfloat16 [8192, 256], P('code'), may hold values from -6 to 6
- kernel_one: bfloat16 [3, 3, 256, 512], replicated, may hold values from -0.125 to 0.125
- kernel_two: bfloat16 [3, 3, 512, 512], replicated, may hold values from -0.09375 to 0.09375
- cotangent: bfloat16 [2, 256, 32, 512], P('clip', ('space', 'code')), may hold values from -6 to 6
Outputs:
- decoded: bfloat16 [2, 256, 32, 512], P('clip', ('space', 'code'))
- grad_one: float32 [3, 3, 256, 512], P(None, None, None, ('space', 'code', 'clip'))
- grad_two: float32 [3, 3, 512, 512], P(None, None, None, ('space', 'code', 'clip'))
- grad_codebook: float32 [8192, 256], P('code')
The draws below stay inside these ranges and needn't reach their ends.
All inputs are finite; a program needn't handle non-finite values.
Results may differ from the reference program's by a relative error of at most 0.02.
Values may be sent and summed in bfloat16 or wider, within the bound.
No kernel may reach another device: no remote copies, remote signals or barrier semaphores. Data moves between devices by JAX's collectives and lax.ppermute only.
A program may use at most 192 MiB of HBM per device.

```python
import math
import jax
import jax.numpy as jnp
from jax import lax

CODES = 8192
CH = 256
WIDTH = 512
COLS = 32
ROWS = 256
CLIPS = 2
N_CLIP = 2


def spiked(drawn, stream_key, source, target, parts, factor):
    owner, partner = [(jnp.arange(drawn.shape[axis_at]) // (drawn.shape[axis_at] // parts)).reshape([-1 if axis == axis_at else 1 for axis in range(drawn.ndim)]) for axis_at in (source, target)]
    chosen = jax.random.permutation(stream_key, parts)[partner]
    strong = (owner == chosen) | (owner == (partner + parts // 2) % parts)
    return jnp.where(strong, factor * drawn, drawn)


def shard_levels(own_key, extent, cuts, low, high):
    loudness = 1.0
    for dim, shards_of in cuts:
        heights = jax.random.uniform(jax.random.fold_in(jax.random.fold_in(own_key, 6), dim), (shards_of,), jnp.float32, low / len(cuts), high / len(cuts))
        loudness = loudness * jnp.repeat(jnp.exp(heights), extent[dim] // shards_of).reshape((-1,) + (1,) * (len(extent) - 1 - dim))
    return loudness


def normal_values(stream_key, extent, scale, most, split=(), kind=jnp.bfloat16):
    factor_of = shard_levels(stream_key, extent, split, -0.22, 0.18) if split else 1.0
    array = jax.random.normal(stream_key, extent, jnp.float32) * scale * factor_of
    return jnp.minimum(jnp.maximum(array, -most), most).astype(kind)


def noise_with(rng, shape, scale, bound, shards, heavy, dtype=jnp.bfloat16):
    values = scale * jax.random.normal(rng, shape, jnp.float32)
    if shards:
        values = values * shard_levels(rng, shape, shards, -0.22, 0.18)
    return jnp.clip(spiked(values, jax.random.fold_in(rng, 3), *heavy), -bound, bound).astype(dtype)


def setup_inputs(seed: int = 0) -> dict:
    splits = jax.random.split(jax.random.key(seed), 6)
    soft_weights = jnp.clip(jnp.exp(math.log(0.029907227) - 4.6038955 * jax.random.uniform(splits[0], (CLIPS, ROWS, COLS, CODES), jnp.float32) ** shard_levels(splits[0], (CLIPS, ROWS, COLS, CODES), ((0, 2), (1, 4), (3, 4)), -0.2, 0.2)), 0.00029945374, 0.029907227).astype(jnp.bfloat16)
    codebook = normal_values(splits[1], (CODES, CH), 1.0, 6.0, ((0, 4),))
    kernel_one = normal_values(splits[2], (3, 3, CH, WIDTH), (9 * CH) ** -0.5, 0.125)
    kernel_two = normal_values(splits[3], (3, 3, WIDTH, WIDTH), (9 * WIDTH) ** -0.5, 0.09375)
    cotangent = noise_with(splits[4], (CLIPS, ROWS, COLS, WIDTH), 1.0, 6.0, ((0, 2), (1, 16)), (1, 3, 16, 2.0))
    return {"soft_weights": soft_weights, "codebook": codebook, "kernel_one": kernel_one, "kernel_two": kernel_two, "cotangent": cotangent}


def pad_grid(field):
    return jnp.pad(field, ((1, 1), (1, 1), (0, 0)))

def taps_forward(padded, kernel):
    height = padded.shape[0] - 2
    breadth = padded.shape[1] - 2
    accum = jnp.zeros((height * breadth, kernel.shape[3]), jnp.float32)
    for first in range(3):
        for second in range(3):
            window = padded[first:first + height, second:second + breadth].reshape(height * breadth, -1)
            accum = accum + jnp.dot(window, kernel[first, second], preferred_element_type=jnp.float32)
    return accum.reshape(height, breadth, -1)

def taps_back(padded, kernel):
    height = padded.shape[0] - 2
    breadth = padded.shape[1] - 2
    accum = jnp.zeros((height * breadth, kernel.shape[2]), jnp.float32)
    for first in range(3):
        for second in range(3):
            window = padded[2 - first:2 - first + height, 2 - second:2 - second + breadth].reshape(height * breadth, -1)
            accum = accum + jnp.dot(window, kernel[first, second].T, preferred_element_type=jnp.float32)
    return accum.reshape(height, breadth, -1)

def kernel_grad(padded, upstream):
    height = upstream.shape[0]
    breadth = upstream.shape[1]
    flat_up = upstream.reshape(height * breadth, -1)
    result = []
    for first in range(3):
        line = []
        for second in range(3):
            window = padded[first:first + height, second:second + breadth].reshape(height * breadth, -1)
            line.append(lax.dot_general(window, flat_up, (((0,), (0,)), ((), ())), preferred_element_type=jnp.float32))
        result.append(jnp.stack(line))
    return jnp.stack(result)

def reference(soft_weights, codebook, kernel_one, kernel_two, cotangent):
    outputs = []
    grad_one = jnp.zeros(kernel_one.shape, jnp.float32)
    grad_two = jnp.zeros(kernel_two.shape, jnp.float32)
    grad_codebook = jnp.zeros(codebook.shape, jnp.float32)
    for clip_index in range(N_CLIP):
        flat = soft_weights[clip_index].reshape(-1, CODES)
        embedded = jnp.dot(flat, codebook, preferred_element_type=jnp.float32).reshape(ROWS, COLS, CH).astype(jnp.bfloat16)
        embed_pad = pad_grid(embedded)
        pre_one = taps_forward(embed_pad, kernel_one)
        hidden = jax.nn.silu(pre_one).astype(jnp.bfloat16)
        hidden_pad = pad_grid(hidden)
        outputs.append(taps_forward(hidden_pad, kernel_two).astype(jnp.bfloat16))
        upstream = cotangent[clip_index]
        grad_two = grad_two + kernel_grad(hidden_pad, upstream)
        grad_hidden = taps_back(pad_grid(upstream), kernel_two)
        sigma = jax.nn.sigmoid(pre_one)
        grad_pre = (grad_hidden * sigma * (1.0 + pre_one * (1.0 - sigma))).astype(jnp.bfloat16)
        grad_one = grad_one + kernel_grad(embed_pad, grad_pre)
        grad_embedded = taps_back(pad_grid(grad_pre), kernel_one).astype(jnp.bfloat16)
        grad_codebook = grad_codebook + lax.dot_general(flat, grad_embedded.reshape(-1, CH), (((0,), (0,)), ((), ())), preferred_element_type=jnp.float32)
    return (jnp.stack(outputs), grad_one, grad_two, grad_codebook)
```

```python
import functools

import jax
import jax.numpy as jnp
from jax import lax
from jax.experimental import pallas as pl
from jax.experimental.pallas import tpu as pltpu
from jax.sharding import PartitionSpec as P

NARROW = jnp.bfloat16
WIDE = jnp.float32


def swap(value, axis, bits):
    return lax.ppermute(value, axis, [(i, i ^ bits) for i in range(lax.axis_size(axis))])


def plus(*terms):
    return sum(term.astype(WIDE) for term in terms).astype(NARROW)


def neighbours(field, width):
    axes = ("space", "code")
    count = lax.axis_size(axes)
    forward = [(i, i + 1) for i in range(count - 1)]
    backward = [(i + 1, i) for i in range(count - 1)]
    low = lax.ppermute(field[-width:], axes, forward)
    high = lax.ppermute(field[:width], axes, backward)
    return jnp.concatenate([low, field, high], axis=0)


def columns(field, offset):
    breadth = field.shape[1]
    if offset == 0:
        return field
    if offset < 0:
        return jnp.pad(field, ((0, 0), (1, 0), (0, 0)))[:, :breadth]
    return jnp.pad(field, ((0, 0), (0, 1), (0, 0)))[:, 1:]


def flat(field):
    return field.reshape(field.shape[0] * field.shape[1], field.shape[2])


def matmul(left, right):
    return jnp.dot(left, right, preferred_element_type=WIDE)


def taps_forward(field, kernel):
    height = field.shape[0] - 2
    wide = jnp.concatenate([columns(field, b - 1) for b in range(3)], axis=2)
    return sum(
        matmul(flat(wide[a : a + height]), kernel[a].reshape(-1, kernel.shape[3])) for a in range(3)
    )


def taps_back(field, turned):
    height = field.shape[0] - 2
    wide = jnp.concatenate([columns(field, 1 - b) for b in range(3)], axis=2)
    return sum(matmul(flat(wide[2 - a : 2 - a + height]), turned[a]) for a in range(3))


def turn(kernel):
    return kernel.transpose(0, 1, 3, 2).reshape(3, 3 * kernel.shape[3], kernel.shape[2])


def kernel_grad_body(
    breadth, pick, own_up, far_up, own_field, far_field, keep_a, send_a, keep_b, send_b, turned
):
    step = pl.program_id(0)
    cells = own_up.shape[0]
    half = pick.shape[0]
    lanes = own_field.shape[1] // 2
    parts = send_a.shape[0] + 1
    tall = half // parts

    @pl.when(step == 0)
    def _():
        for source, ref in enumerate((own_up, far_up)):
            across = lax.dot_general(
                pick[...], ref[...], (((1,), (1,)), ((), ())), preferred_element_type=WIDE
            )
            column = lax.broadcasted_iota(jnp.int32, across.shape, 1) % breadth
            after = jnp.where(column == breadth - 1, 0.0, pltpu.roll(across, cells - 1, 1))
            before = jnp.where(column == 0, 0.0, pltpu.roll(across, 1, 1))
            for b, value in enumerate((after, across, before)):
                turned[source, b * half : (b + 1) * half, :] = value.astype(NARROW)

    rows = pl.ds(pl.multiple_of(step * breadth, breadth), cells)
    total = matmul(turned[0], own_field[rows, :]) + matmul(turned[1], far_field[rows, :])
    total = total.astype(NARROW)
    short = tall // 2
    for b in range(3):
        for k in range(parts):
            base = b * half + k * tall
            block = total[base : base + tall]
            if k == 0:
                keep_a[0, b] = block[:, :lanes]
            else:
                send_a[k - 1, 0, b] = block[:, :lanes]
            keep_b[0, b, k] = block[:short, lanes:]
            send_b[0, b, k] = block[short:, lanes:]


def kernel_grad(pick, own_up, far_up, own_field, far_field, breadth, parts):
    half = pick.shape[0]
    cells = own_up.shape[0]
    inputs = own_field.shape[1]
    lanes = inputs // 2
    tall = half // parts
    whole = lambda array: pl.BlockSpec(array.shape, lambda a: (0, 0))
    operands = (pick, own_up, far_up, own_field, far_field)
    shapes = (
        ((3, 3, tall, lanes), (1, 3, tall, lanes), lambda a: (a, 0, 0, 0)),
        (
            (parts - 1, 3, 3, tall, lanes),
            (parts - 1, 1, 3, tall, lanes),
            lambda a: (0, a, 0, 0, 0),
        ),
        ((3, 3, parts, tall // 2, lanes), (1, 3, parts, tall // 2, lanes), lambda a: (a, 0, 0, 0, 0)),
        ((3, 3, parts, tall // 2, lanes), (1, 3, parts, tall // 2, lanes), lambda a: (a, 0, 0, 0, 0)),
    )
    return pl.pallas_call(
        functools.partial(kernel_grad_body, breadth),
        grid=(3,),
        in_specs=[whole(array) for array in operands],
        out_specs=[pl.BlockSpec(block, index) for _, block, index in shapes],
        out_shape=[jax.ShapeDtypeStruct(shape, NARROW) for shape, _, _ in shapes],
        scratch_shapes=[pltpu.VMEM((2, 3 * half, cells), NARROW)],
        compiler_params=pltpu.CompilerParams(vmem_limit_bytes=40 * 1024 * 1024),
        cost_estimate=pl.CostEstimate(
            flops=2 * 2 * 9 * half * cells * inputs,
            bytes_accessed=9 * half * inputs * 2 + 4 * cells * inputs * 2,
            transcendentals=0,
        ),
    )(*operands)


def spread(parts_of):
    keep_a, send_a, keep_b, send_b = parts_of
    parts = send_a.shape[0] + 1
    got = [swap(send_a[k - 1], "space", 2 * k) for k in range(1, parts)]
    from_clip = swap(send_b, "clip", 1)
    first = plus(keep_a, *got)
    short = first.shape[2] // 2
    first = plus(first[:, :, :short], swap(first[:, :, short:], "clip", 1))
    second = plus(keep_b, from_clip)
    got = [swap(second[:, :, k], "space", 2 * k) for k in range(1, parts)]
    second = plus(second[:, :, 0], *got)
    joined = jnp.concatenate([first, second], axis=3)
    grain = joined.shape[2] // 4
    piece = lambda k: joined[:, :, k * grain : (k + 1) * grain]
    middle = plus(piece(2), swap(piece(3), "code", 1))
    near = swap(piece(1), "code", 1)
    far = swap(middle, "code", 2)
    total = piece(0).astype(WIDE) + near.astype(WIDE) + far.astype(WIDE)
    return total.transpose(0, 1, 3, 2)


def own_channels(width):
    parts = lax.axis_size("space") // 2
    space = lax.axis_index("space")
    code = lax.axis_index("code")
    clip = lax.axis_index("clip")
    grain = width // (parts * 16)
    index = jnp.arange(width // 2)
    inner = index % grain
    d_code = (index // grain) % 4
    d_clip = (index // (grain * 4)) % 2
    d_space = index // (grain * 8)
    owner = ((space ^ (2 * d_space)) * 4 + (code ^ d_code)) * 2 + (clip ^ d_clip)
    channel = owner * grain + inner
    return (channel[:, None] == jnp.arange(width)[None, :]).astype(NARROW)


def sum_over_tiles(term):
    core = lax.axis_index("space") % 2
    half = term.shape[0] // 2
    mine = lax.dynamic_slice_in_dim(term, core * half, half, 0)
    other = lax.dynamic_slice_in_dim(term, (1 - core) * half, half, 0)
    mine = plus(mine, swap(other, "space", 1))
    stages = []
    bits = 2
    while bits < lax.axis_size("space"):
        stages.append(("space", bits))
        bits *= 2
    first, second = mine[: half // 2], mine[half // 2 :]
    for one, two in zip(stages + [("clip", 1)], [("clip", 1)] + stages):
        first, second = lax.optimization_barrier((first, second))
        got_one, got_two = swap(first, *one), swap(second, *two)
        first, second = plus(first, got_one), plus(second, got_two)
    mine = lax.optimization_barrier(jnp.concatenate([first, second], axis=0))
    other = swap(mine, "space", 1)
    low = jnp.where(core == 0, mine, other)
    high = jnp.where(core == 0, other, mine)
    return jnp.concatenate([low, high], axis=0).astype(WIDE)


def on_device(soft_weights, codebook, kernel_one, kernel_two, cotangent):
    weights = soft_weights[0]
    upstream = cotangent[0]
    own_rows, breadth, width = upstream.shape
    parts = lax.axis_size("space") // 2
    code = lax.axis_index("code")
    place = lax.axis_index("space") * 4 + code
    last = lax.axis_size("space") * 4 - 1

    def tile(k):
        return flat(lax.dynamic_slice_in_dim(weights, (code ^ k) * own_rows, own_rows, 0))

    partial = [matmul(tile(k), codebook) for k in (3, 2, 1, 0)][::-1]
    middle = plus(partial[2], swap(partial[3].astype(NARROW), "code", 1))
    near = swap(partial[1].astype(NARROW), "code", 1)
    far = swap(middle, "code", 2)
    embedded = plus(partial[0], near, far).reshape(own_rows, breadth, -1)

    pick = own_channels(width)
    far_upstream = swap(flat(upstream), "space", 1)
    grad_hidden = taps_back(neighbours(upstream, 2), turn(kernel_two))
    turned_one = turn(kernel_one)

    embed_pad = neighbours(embedded, 2)
    pre_one = taps_forward(embed_pad, kernel_one)
    row = lax.broadcasted_iota(jnp.int32, (own_rows + 2, breadth, 1), 0)
    inside = flat(((row > 0) | (place > 0)) & ((row <= own_rows) | (place < last)))
    sigma = jax.nn.sigmoid(pre_one)
    hidden = jnp.where(inside, pre_one * sigma, 0.0).astype(NARROW)
    grad_pre = jnp.where(
        inside, grad_hidden * sigma * (1.0 + pre_one * (1.0 - sigma)), 0.0
    ).astype(NARROW)
    grad_embedded = taps_back(grad_pre.reshape(own_rows + 2, breadth, -1), turned_one).astype(NARROW)

    across = swap(grad_embedded, "code", 2)
    beside = swap(grad_embedded, "code", 1)
    corner = swap(across, "code", 1)

    own_pre = grad_pre[breadth:-breadth]
    far_hidden = swap(hidden, "space", 1)
    far_pre = swap(own_pre, "space", 1)
    field = flat(embed_pad[1:-1])
    far_field = swap(field, "space", 1)
    grad_two = spread(
        kernel_grad(pick, flat(upstream), far_upstream, hidden, far_hidden, breadth, parts)
    )
    grad_one = spread(kernel_grad(pick, own_pre, far_pre, field, far_field, breadth, parts))
    decoded = taps_forward(hidden.reshape(own_rows + 2, breadth, -1), kernel_two).astype(NARROW)

    term = sum(
        lax.dot_general(tile(k), piece, (((0,), (0,)), ((), ())), preferred_element_type=WIDE)
        for k, piece in enumerate((grad_embedded, beside, across, corner))
    )
    grad_codebook = sum_over_tiles(term)
    return (decoded.reshape(upstream.shape)[None], grad_one, grad_two, grad_codebook)


def solution(mesh):
    in_specs = (
        P("clip", "space", None, "code"),
        P("code", None),
        P(),
        P(),
        P("clip", ("space", "code"), None, None),
    )
    out_specs = (
        P("clip", ("space", "code"), None, None),
        P(None, None, None, ("space", "code", "clip")),
        P(None, None, None, ("space", "code", "clip")),
        P("code", None),
    )
    return jax.shard_map(
        on_device, mesh=mesh, in_specs=in_specs, out_specs=out_specs, check_vma=False
    )
```

```python
import functools

import jax
import jax.numpy as jnp
from jax import lax
from jax.experimental import pallas as pl
from jax.experimental.pallas import tpu as pltpu
from jax.sharding import PartitionSpec as P

NARROW = jnp.bfloat16
WIDE = jnp.float32
COST = 8
SMALL, LARGE, WHOLE = 16 * 1024 * 1024, 24 * 1024 * 1024, 56 * 1024 * 1024


def swap(value, axis, bits, name):
    with jax.named_scope(name):
        return lax.ppermute(value, axis, [(i, i ^ bits) for i in range(lax.axis_size(axis))])


def after(value, *others):
    return lax.optimization_barrier((value, *others))[0]


def plus(*terms):
    return sum(term.astype(WIDE) for term in terms).astype(NARROW)


def edges(top, bottom, name):
    axes = ("space", "code")
    count = lax.axis_size(axes)
    forward = [(i, i + 1) for i in range(count - 1)]
    backward = [(i + 1, i) for i in range(count - 1)]
    with jax.named_scope(name):
        low = lax.ppermute(bottom, axes, forward)
        high = lax.ppermute(top, axes, backward)
    return low, high


def matmul(left, right):
    return jnp.dot(left, right, preferred_element_type=WIDE)


def matmul_turned(left, right):
    return lax.dot_general(left, right, (((1,), (1,)), ((), ())), preferred_element_type=WIDE)


def step_columns(value, offset, breadth):
    if offset == 0:
        return value
    count = value.shape[0]
    column = lax.broadcasted_iota(jnp.int32, value.shape, 0) % breadth
    moved = pltpu.roll(value, (-offset) % count, 0)
    return jnp.where(column == (0 if offset < 0 else breadth - 1), 0.0, moved)


def call(body, operands, outs, flops, scratch=(), limit=SMALL, spaces=None):
    local = pl.BlockSpec(memory_space=pltpu.VMEM)
    return pl.pallas_call(
        body,
        in_specs=[pl.BlockSpec(memory_space=space) for space in spaces] if spaces else [local] * len(operands),
        out_specs=[local] * len(outs),
        out_shape=[jax.ShapeDtypeStruct(shape, dtype) for shape, dtype in outs],
        scratch_shapes=list(scratch),
        compiler_params=pltpu.CompilerParams(vmem_limit_bytes=limit),
        cost_estimate=pl.CostEstimate(flops=flops // COST, bytes_accessed=1, transcendentals=0),
    )(*operands)


def fuse(*tasks):
    spans = [(len(operands), len(outs), len(scratch)) for _, operands, outs, scratch in tasks]
    counts = [sum(span[k] for span in spans) for k in range(3)]

    def body(*refs):
        at = [0, counts[0], counts[0] + counts[1]]
        for (task, *_), span in zip(tasks, spans):
            picked = []
            for k in range(3):
                picked += refs[at[k] : at[k] + span[k]]
                at[k] += span[k]
            task(*picked)

    operands = [operand for task in tasks for operand in task[1]]
    results = list(
        call(
            body,
            operands,
            [out for task in tasks for out in task[2]],
            8 * 10**8,
            [item for task in tasks for item in task[3]],
            spaces=[pltpu.SMEM if item.dtype == jnp.int32 else pltpu.VMEM for item in operands],
        )
    )
    return [[results.pop(0) for _ in range(span[1])] for span in spans]


def lookup_body(count, edge, order, weights, codebook, *refs):
    outs, total = refs[:-1], refs[-1]
    shard, step = pl.program_id(0), pl.program_id(1)
    last = pl.num_programs(1) - 1
    term = matmul(weights[...], codebook[...])

    @pl.when(step == 0)
    def _():
        total[...] = term

    @pl.when(step > 0)
    def _():
        total[...] += term

    for k in range(count):

        @pl.when((step == last) & (shard == k))
        def _():
            if len(outs) == 1:
                ends, inner = outs[0].at[: 2 * edge], outs[0].at[2 * edge :]
            else:
                ends, inner = outs[2 * k], outs[2 * k + 1]
            ends[:edge] = total[:edge].astype(NARROW)
            ends[edge:] = total[-edge:].astype(NARROW)
            inner[...] = total[edge:-edge].astype(NARROW)


def lookup(places, info, weights, codebook, cells, edge, split):
    codes, inner = codebook.shape
    count = len(places)
    first = places[0]
    rows = [cells] if count == 1 else [2 * edge, cells - 2 * edge] * count
    return pl.pallas_call(
        functools.partial(lookup_body, count, edge),
        grid_spec=pltpu.PrefetchScalarGridSpec(
            num_scalar_prefetch=1,
            grid=(count, split),
            in_specs=[
                pl.BlockSpec((cells, codes // split), lambda i, j, order: (order[first + i], j)),
                pl.BlockSpec((codes // split, inner), lambda i, j, order: (j, 0)),
            ],
            out_specs=[pl.BlockSpec((height, inner), lambda i, j, order: (0, 0)) for height in rows],
            scratch_shapes=[pltpu.VMEM((cells, inner), WIDE)],
        ),
        out_shape=[jax.ShapeDtypeStruct((height, inner), NARROW) for height in rows],
        compiler_params=pltpu.CompilerParams(vmem_limit_bytes=WHOLE),
        cost_estimate=pl.CostEstimate(
            flops=2 * count * cells * codebook.size // COST, bytes_accessed=1, transcendentals=0
        ),
    )(info, weights, codebook)


def upstream_body(breadth, own, low, high, kernel, out, padded):
    edge = low.shape[0]
    cells = own.shape[0]
    tall = out.shape[0]
    padded[:edge] = low[...]
    padded[edge : edge + cells] = own[...]
    padded[edge + cells :] = high[...]
    for b in (1, 0, 2):
        total = sum(
            matmul_turned(padded[(2 - a) * breadth : (2 - a) * breadth + tall], kernel[a, b])
            for a in range(3)
        )
        total = step_columns(total, 1 - b, breadth)
        out[...] = total if b == 1 else out[...] + total


def upstream_back(own, low, high, kernel, breadth):
    cells, width = own.shape
    return call(
        functools.partial(upstream_body, breadth),
        (own, low, high, kernel),
        [((cells + 2 * breadth, kernel.shape[2]), WIDE)],
        2 * cells * kernel.size,
        [pltpu.VMEM((cells + 2 * low.shape[0], width), NARROW)],
    )[0]


def head_body(
    breadth, info, low, top, inner, bottom, high, kernel, grad_hidden, hidden, own_pre, field, grad, padded, grad_pre
):
    cells = grad.shape[0]
    tall = hidden.shape[0]
    at = 0
    for part in (low, top, inner, bottom, high):
        padded[at : at + part.shape[0]] = part[...]
        at += part.shape[0]
    field[...] = padded[breadth : breadth + tall]
    pre = sum(
        step_columns(
            sum(matmul(padded[a * breadth : a * breadth + tall], kernel[a, b]) for a in range(3)),
            b - 1,
            breadth,
        )
        for b in (1, 0, 2)
    )
    row = lax.broadcasted_iota(jnp.int32, pre.shape, 0)
    inside = ((row >= breadth) | (info[4] > 0)) & ((row < tall - breadth) | (info[5] > 0))
    sigma = 1.0 / (1.0 + jnp.exp(-pre))
    hidden[...] = jnp.where(inside, pre * sigma, 0.0).astype(NARROW)
    slope = grad_hidden[...] * (sigma * (1.0 + pre * (1.0 - sigma)))
    grad_pre[...] = jnp.where(inside, slope, 0.0).astype(NARROW)
    own_pre[...] = grad_pre[breadth : breadth + cells]
    total = sum(
        step_columns(
            sum(
                matmul_turned(
                    grad_pre[(2 - a) * breadth : (2 - a) * breadth + cells], kernel[a, b]
                )
                for a in range(3)
            ),
            1 - b,
            breadth,
        )
        for b in (1, 0, 2)
    )
    grad[...] = total.astype(NARROW)


def head(info, parts, kernel, grad_hidden, breadth):
    inputs = parts[0].shape[1]
    tall, width = grad_hidden.shape
    cells = tall - 2 * breadth
    return call(
        functools.partial(head_body, breadth),
        (info, *parts, kernel, grad_hidden),
        [((tall, width), NARROW), ((cells, width), NARROW), ((tall, inputs), NARROW), ((cells, inputs), NARROW)],
        4 * cells * kernel.size,
        [pltpu.VMEM((tall + 2 * breadth, inputs), NARROW), pltpu.VMEM((tall, width), NARROW)],
        spaces=(pltpu.SMEM,) + (pltpu.VMEM,) * 7,
    )


def decode_body(breadth, hidden, kernel, out):
    cells = out.shape[0]
    total = sum(
        step_columns(
            sum(matmul(hidden[a * breadth : a * breadth + cells], kernel[a, b]) for a in range(3)),
            b - 1,
            breadth,
        )
        for b in (1, 0, 2)
    )
    out[...] = total.astype(NARROW)


def decode(hidden, kernel, breadth):
    tall = hidden.shape[0]
    return call(
        functools.partial(decode_body, breadth),
        (hidden, kernel),
        [((tall - 2 * breadth, kernel.shape[3]), NARROW)],
        2 * (tall - 2 * breadth) * kernel.size,
    )[0]


def term_of(info, place, weights, field):
    cells = field.shape[0]
    rows = pl.ds(pl.multiple_of(info[place] * cells, cells), cells)
    return lax.dot_general(
        weights[rows, :], field[...], (((0,), (0,)), ((), ())), preferred_element_type=WIDE
    )


def book_start_body(info, weights, own, beside, across, out):
    out[...] = term_of(info, 3, weights, own)
    out[...] += term_of(info, 2, weights, beside)
    out[...] += term_of(info, 1, weights, across)


def book_end_body(info, weights, corner, base, mine, other, total):
    total[...] = base[...] + term_of(info, 0, weights, corner)
    half = mine.shape[0]
    core = info[6]
    mine[...] = total[pl.ds(pl.multiple_of(core * half, half), half), :].astype(NARROW)
    other[...] = total[pl.ds(pl.multiple_of((1 - core) * half, half), half), :].astype(NARROW)


def book_start(info, weights, own, beside, across):
    shape = (weights.shape[1], own.shape[1])
    return call(
        book_start_body,
        (info, weights, own, beside, across),
        [(shape, WIDE)],
        6 * weights.shape[1] * own.size,
        spaces=(pltpu.SMEM,) + (pltpu.VMEM,) * 4,
    )[0]


def book_end(info, weights, corner, base):
    half = (base.shape[0] // 2, base.shape[1])
    return (
        book_end_body,
        (info, weights, corner, base),
        [(half, NARROW), (half, NARROW)],
        [pltpu.VMEM(base.shape, WIDE)],
    )


def halves_body(mine, got, first, second):
    half = first.shape[0]
    first[...] = plus(mine[:half], got[:half])
    second[...] = plus(mine[half:], got[half:])


def halves(mine, got):
    half = (mine.shape[0] // 2, mine.shape[1])
    return halves_body, (mine, got), [(half, NARROW), (half, NARROW)], []


def pair_body(first, got_first, second, got_second, *outs):
    half = first.shape[0]
    if len(outs) == 2:
        outs[0][...] = plus(first[...], got_first[...])
        outs[1][...] = plus(second[...], got_second[...])
    else:
        outs[0][:half] = plus(first[...], got_first[...])
        outs[0][half:] = plus(second[...], got_second[...])


def pair(first, got_first, second, got_second, joined):
    rows, lanes = first.shape
    outs = [((2 * rows, lanes), NARROW)] if joined else [((rows, lanes), NARROW)] * 2
    return pair_body, (first, got_first, second, got_second), outs, []


def kernel_grad_part(breadth, at, pick, own_up, far_up, own_field, far_field, outs, turned):
    keep_a, send_a, keep_b, send_b = outs
    cells = own_up.shape[0]
    half = pick.shape[0]
    lanes = own_field.shape[1] // 2
    parts = send_a.shape[0] + 1
    tall = half // parts
    short = tall // 2
    for source, ref in enumerate((own_up, far_up)):
        across = matmul_turned(pick[...], ref[...])
        column = lax.broadcasted_iota(jnp.int32, across.shape, 1) % breadth
        later = jnp.where(column == breadth - 1, 0.0, pltpu.roll(across, cells - 1, 1))
        sooner = jnp.where(column == 0, 0.0, pltpu.roll(across, 1, 1))
        for b, value in enumerate((later, across, sooner)):
            turned[source, b * half : (b + 1) * half, :] = value.astype(NARROW)

    @pl.loop(0, 3)
    def _(a):
        rows = pl.ds(pl.multiple_of(a * breadth, breadth), cells)
        total = matmul(turned[0], own_field[rows, :]) + matmul(turned[1], far_field[rows, :])
        total = total.astype(NARROW)
        for b in range(3):
            for k in range(parts):
                base = b * half + k * tall
                block = total[base : base + tall]
                if k == 0:
                    keep_a[a, b, :, at : at + lanes] = block[:, :lanes]
                else:
                    send_a[k - 1, a, b, :, at : at + lanes] = block[:, :lanes]
                keep_b[a, b, k, :, at : at + lanes] = block[:short, lanes:]
                send_b[a, b, k, :, at : at + lanes] = block[short:, lanes:]


def kernel_grads_body(breadth, pick, *refs):
    outs, turned = refs[8:12], refs[-1]
    kernel_grad_part(breadth, 0, pick, *refs[:4], outs, turned)
    kernel_grad_part(breadth, refs[2].shape[1] // 2, pick, *refs[4:8], outs, turned)


def kernel_grads(pick, two, one, breadth, parts):
    half = pick.shape[0]
    cells = two[0].shape[0]
    tall = half // parts
    lanes = (two[2].shape[1] + one[2].shape[1]) // 2
    shapes = [
        (3, 3, tall, lanes),
        (parts - 1, 3, 3, tall, lanes),
        (3, 3, parts, tall // 2, lanes),
        (3, 3, parts, tall // 2, lanes),
    ]
    return call(
        functools.partial(kernel_grads_body, breadth),
        (pick, *two, *one),
        [(shape, NARROW) for shape in shapes],
        36 * half * (two[2].size + one[2].size),
        [pltpu.VMEM((2, 3 * half, cells), NARROW)],
        limit=LARGE,
    )


def own_channels(width):
    parts = lax.axis_size("space") // 2
    space = lax.axis_index("space")
    code = lax.axis_index("code")
    clip = lax.axis_index("clip")
    grain = width // (parts * 16)
    index = jnp.arange(width // 2)
    inner = index % grain
    d_code = (index // grain) % 4
    d_clip = (index // (grain * 4)) % 2
    d_space = index // (grain * 8)
    owner = ((space ^ (2 * d_space)) * 4 + (code ^ d_code)) * 2 + (clip ^ d_clip)
    channel = owner * grain + inner
    return (channel[:, None] == jnp.arange(width)[None, :]).astype(NARROW)


def turn_body(keep_a, keep_b, got_b, *refs):
    keep_first, send_first, keep_second, send_second = refs[-4:]
    got_a = refs[:-4]
    short = keep_first.shape[2]
    for a in range(3):
        for b in range(3):
            total = plus(keep_a[a, b], *[got[a, b] for got in got_a])
            keep_first[a, b] = total[:short]
            send_first[a, b] = total[short:]
            total = plus(keep_b[a, b], got_b[a, b])
            keep_second[a, b] = total[0]
            for k in range(1, total.shape[0]):
                send_second[k - 1, a, b] = total[k]


def along_body(keep_first, got_first, keep_second, *refs):
    outs = refs[-4:] if refs[-1].shape[2] * 4 == keep_first.shape[2] else refs[-1:]
    got_second = refs[: -len(outs)]
    lanes = keep_first.shape[3]
    grain = keep_first.shape[2] // len(outs)
    for a in range(3):
        for b in range(3):
            first = plus(keep_first[a, b], got_first[a, b])
            second = plus(keep_second[a, b], *[got[a, b] for got in got_second])
            for k, out in enumerate(outs):
                out[a, b, :, :lanes] = first[k * grain : (k + 1) * grain]
                out[a, b, :, lanes:] = second[k * grain : (k + 1) * grain]


class Spread:
    def __init__(self, parts_of, name):
        self.keep_a, send_a, self.keep_b, send_b = parts_of
        self.name = name
        self.parts = send_a.shape[0] + 1
        self.got_a = [swap(send_a[k - 1], "space", 2 * k, name + "_a1") for k in range(1, self.parts)]
        self.got_b = swap(send_b, "clip", 1, name + "_b1")

    def turn(self):
        tall, lanes = self.keep_a.shape[2:]
        shape = (3, 3, tall // 2, lanes)
        outs = [(shape, NARROW)] * 3 + [((self.parts - 1,) + shape, NARROW)]
        return turn_body, (self.keep_a, self.keep_b, self.got_b, *self.got_a), outs, []

    def turned(self, outs):
        self.first, send_first, self.second, send_second = outs
        self.got_a = swap(send_first, "clip", 1, self.name + "_a2")
        self.got_b = [
            swap(send_second[k - 1], "space", 2 * k, self.name + "_b2") for k in range(1, self.parts)
        ]

    def along(self):
        rows, lanes = self.first.shape[2:]
        outs = [((3, 3, rows, 2 * lanes), NARROW)]
        if rows % 64 == 0:
            outs = [((3, 3, rows // 4, 2 * lanes), NARROW)] * 4
        return along_body, (self.first, self.got_a, self.second, *self.got_b), outs, []

    def sent(self, outs):
        if len(outs) == 1:
            grain = outs[0].shape[2] // 4
            outs = [outs[0][:, :, k * grain : (k + 1) * grain] for k in range(4)]
        self.last = outs[0]
        self.got = [swap(outs[k], "code", k, self.name + "_z") for k in (2, 1, 3)]

    def done(self, split):
        total = sum(got.astype(WIDE) for got in self.got) + self.last.astype(WIDE)
        total = total.transpose(0, 1, 3, 2)
        half = total.shape[2] // 2
        one = jnp.concatenate([total[:, :, split:half], total[:, :, half + split :]], axis=2)
        two = jnp.concatenate([total[:, :, :split], total[:, :, half : half + split]], axis=2)
        return one, two


def on_device(soft_weights, codebook, kernel_one, kernel_two, cotangent):
    weights = soft_weights[0]
    weights = weights.reshape(-1, weights.shape[2])
    own_rows, breadth, width = cotangent.shape[1:]
    upstream = cotangent[0]
    cells = own_rows * breadth
    own_up = upstream.reshape(cells, width)
    parts = lax.axis_size("space") // 2
    code = lax.axis_index("code")
    space = lax.axis_index("space")
    place = space * 4 + code
    last = lax.axis_size("space") * 4 - 1
    flat = lambda field: field.reshape(-1, field.shape[2])
    info = jnp.stack([code ^ 3, code ^ 2, code ^ 1, code, place, last - place, space % 2, 0])
    info = info.astype(jnp.int32)

    edge = 2 * breadth
    (third,) = lookup((0,), info, weights, codebook, cells, edge, 2)
    from_pair = swap(third, "code", 1, "look_z1")
    upstream = after(own_up, third)
    cot_low, cot_high = edges(upstream[:edge], upstream[-edge:], "cot_edge")
    shards = lookup((1, 2, 3), info, weights, after(codebook, third), cells, edge, 1)
    pick = after(own_channels(width), shards[0])
    (second_ends, second, beside_ends, beside, own_ends, own), pick, cot_low, cot_high = (
        lax.optimization_barrier((shards, pick, cot_low, cot_high))
    )
    middle_ends = plus(second_ends, from_pair[: 2 * edge])
    far_ends = swap(middle_ends, "code", 2, "look_ends")
    near_ends = swap(beside_ends, "code", 1, "look_near_ends")
    middle = plus(after(second, middle_ends), from_pair[2 * edge :])
    far = swap(middle, "code", 2, "look_z2")
    near = swap(after(beside, middle), "code", 1, "look_near")
    grad_hidden = upstream_back(after(own_up, middle), cot_low, cot_high, kernel_two, breadth)
    far_up = swap(after(own_up, middle), "space", 1, "cot_core")
    own_ends, own, grad_hidden, far_up = lax.optimization_barrier(
        (own_ends, own, grad_hidden, far_up)
    )
    part = lambda k: slice(k * edge, (k + 1) * edge)
    top, bottom = [
        plus(own_ends[part(k)], near_ends[part(k)], far_ends[part(k)]) for k in range(2)
    ]
    low, high = edges(top, bottom, "embed_edge")
    inner = plus(after(own, top, bottom), near, far)
    hidden, own_pre, field, grad_embedded = head(
        info, (low, top, inner, bottom, high), kernel_one, grad_hidden, breadth
    )

    across = swap(grad_embedded, "code", 2, "ge_z2")
    beside = swap(grad_embedded, "code", 1, "ge_z1")
    far_hidden = swap(hidden, "space", 1, "hidden_core")
    far_pre = swap(own_pre, "space", 1, "pre_core")
    far_field = swap(field, "space", 1, "field_core")
    grads = kernel_grads(
        pick,
        (own_up, far_up, hidden, far_hidden),
        (own_pre, far_pre, field, far_field),
        breadth,
        parts,
    )
    across, beside = after((across, beside), grads[0])
    grads = Spread(grads, "grads")
    corner = swap(across, "code", 1, "ge_z3")
    term = book_start(info, weights, grad_embedded, beside, across)
    ((mine, other),) = fuse(book_end(info, weights, corner, term))
    got = swap(other, "space", 1, "book_core")
    ((first, second),) = fuse(halves(mine, got))

    stages = []
    bits = 2
    while bits < lax.axis_size("space"):
        stages.append(("space", bits))
        bits *= 2
    ways = list(zip(stages + [("clip", 1)], [("clip", 1)] + stages))
    for k, (way, back) in enumerate(ways):
        got_first, got_second = swap(first, *way, "book_a"), swap(second, *back, "book_b")
        task = pair(first, got_first, second, got_second, k == len(ways) - 1)
        if k == 0:
            outs, (first, second) = fuse(grads.turn(), task)
            grads.turned(outs)
        elif k < len(ways) - 1:
            ((first, second),) = fuse(task)
        else:
            decoded = decode(after(hidden, first, second), kernel_two, breadth)
            task = (task[0], (after(first, decoded),) + task[1][1:]) + task[2:]
            outs, (mine,) = fuse(grads.along(), task)
            grads.sent(outs)
    other = swap(mine, "space", 1, "book_back")
    core = space % 2
    low = jnp.where(core == 0, mine, other)
    high = jnp.where(core == 0, other, mine)
    grad_codebook = jnp.concatenate([low, high], axis=0).astype(WIDE)
    grad_one, grad_two = grads.done(width // 2)
    return (decoded.reshape(cotangent.shape), grad_one, grad_two, grad_codebook)


def solution(mesh):
    in_specs = (
        P("clip", "space", None, "code"),
        P("code", None),
        P(),
        P(),
        P("clip", ("space", "code"), None, None),
    )
    out_specs = (
        P("clip", ("space", "code"), None, None),
        P(None, None, None, ("space", "code", "clip")),
        P(None, None, None, ("space", "code", "clip")),
        P("code", None),
    )
    return jax.shard_map(
        on_device, mesh=mesh, in_specs=in_specs, out_specs=out_specs, check_vma=False
    )
```

```python
import functools

import jax
import jax.numpy as jnp
from jax import lax
from jax.experimental import pallas as pl
from jax.experimental.pallas import tpu as pltpu
from jax.sharding import PartitionSpec as P

NARROW = jnp.bfloat16
WIDE = jnp.float32
COST = 8
SMALL, LARGE, WHOLE = 16 * 1024 * 1024, 24 * 1024 * 1024, 56 * 1024 * 1024


def swap(value, axis, bits, name):
    with jax.named_scope(name):
        return lax.ppermute(value, axis, [(i, i ^ bits) for i in range(lax.axis_size(axis))])


def after(value, *others):
    return lax.optimization_barrier((value, *others))[0]


def plus(*terms):
    return sum(term.astype(WIDE) for term in terms).astype(NARROW)


def edges(top, bottom, name):
    axes = ("space", "code")
    count = lax.axis_size(axes)
    forward = [(i, i + 1) for i in range(count - 1)]
    backward = [(i + 1, i) for i in range(count - 1)]
    with jax.named_scope(name):
        low = lax.ppermute(bottom, axes, forward)
        high = lax.ppermute(top, axes, backward)
    return low, high


def matmul(left, right):
    return jnp.dot(left, right, preferred_element_type=WIDE)


def matmul_turned(left, right):
    return lax.dot_general(left, right, (((1,), (1,)), ((), ())), preferred_element_type=WIDE)


def step_columns(value, offset, breadth):
    if offset == 0:
        return value
    count = value.shape[0]
    column = lax.broadcasted_iota(jnp.int32, value.shape, 0) % breadth
    moved = pltpu.roll(value, (-offset) % count, 0)
    return jnp.where(column == (0 if offset < 0 else breadth - 1), 0.0, moved)


def call(body, operands, outs, flops, scratch=(), limit=SMALL, spaces=None):
    local = pl.BlockSpec(memory_space=pltpu.VMEM)
    return pl.pallas_call(
        body,
        in_specs=[pl.BlockSpec(memory_space=space) for space in spaces] if spaces else [local] * len(operands),
        out_specs=[local] * len(outs),
        out_shape=[jax.ShapeDtypeStruct(shape, dtype) for shape, dtype in outs],
        scratch_shapes=list(scratch),
        compiler_params=pltpu.CompilerParams(vmem_limit_bytes=limit),
        cost_estimate=pl.CostEstimate(flops=flops // COST, bytes_accessed=1, transcendentals=0),
    )(*operands)


def fuse(*tasks):
    spans = [(len(operands), len(outs), len(scratch)) for _, operands, outs, scratch in tasks]
    counts = [sum(span[k] for span in spans) for k in range(3)]

    def body(*refs):
        at = [0, counts[0], counts[0] + counts[1]]
        for (task, *_), span in zip(tasks, spans):
            picked = []
            for k in range(3):
                picked += refs[at[k] : at[k] + span[k]]
                at[k] += span[k]
            task(*picked)

    operands = [operand for task in tasks for operand in task[1]]
    results = list(
        call(
            body,
            operands,
            [out for task in tasks for out in task[2]],
            8 * 10**8,
            [item for task in tasks for item in task[3]],
            spaces=[pltpu.SMEM if item.dtype == jnp.int32 else pltpu.VMEM for item in operands],
        )
    )
    return [[results.pop(0) for _ in range(span[1])] for span in spans]


def lookup_body(count, edge, order, weights, codebook, *refs):
    outs, total = refs[:-1], refs[-1]
    shard, step = pl.program_id(0), pl.program_id(1)
    last = pl.num_programs(1) - 1
    term = matmul(weights[...], codebook[...])

    @pl.when(step == 0)
    def _():
        total[...] = term

    @pl.when(step > 0)
    def _():
        total[...] += term

    for k in range(count):

        @pl.when((step == last) & (shard == k))
        def _():
            if len(outs) == 1:
                ends, inner = outs[0].at[: 2 * edge], outs[0].at[2 * edge :]
            else:
                ends, inner = outs[2 * k], outs[2 * k + 1]
            ends[:edge] = total[:edge].astype(NARROW)
            ends[edge:] = total[-edge:].astype(NARROW)
            inner[...] = total[edge:-edge].astype(NARROW)


def lookup(places, info, weights, codebook, cells, edge, split):
    codes, inner = codebook.shape
    count = len(places)
    first = places[0]
    rows = [cells] if count == 1 else [2 * edge, cells - 2 * edge] * count
    return pl.pallas_call(
        functools.partial(lookup_body, count, edge),
        grid_spec=pltpu.PrefetchScalarGridSpec(
            num_scalar_prefetch=1,
            grid=(count, split),
            in_specs=[
                pl.BlockSpec((cells, codes // split), lambda i, j, order: (order[first + i], j)),
                pl.BlockSpec((codes // split, inner), lambda i, j, order: (j, 0)),
            ],
            out_specs=[pl.BlockSpec((height, inner), lambda i, j, order: (0, 0)) for height in rows],
            scratch_shapes=[pltpu.VMEM((cells, inner), WIDE)],
        ),
        out_shape=[jax.ShapeDtypeStruct((height, inner), NARROW) for height in rows],
        compiler_params=pltpu.CompilerParams(vmem_limit_bytes=WHOLE),
        cost_estimate=pl.CostEstimate(
            flops=2 * count * cells * codebook.size // COST, bytes_accessed=1, transcendentals=0
        ),
    )(info, weights, codebook)


def upstream_body(breadth, own, low, high, kernel, out, padded):
    edge = low.shape[0]
    cells = own.shape[0]
    tall = out.shape[0]
    padded[:edge] = low[...]
    padded[edge : edge + cells] = own[...]
    padded[edge + cells :] = high[...]
    for b in (1, 0, 2):
        total = sum(
            matmul_turned(padded[(2 - a) * breadth : (2 - a) * breadth + tall], kernel[a, b])
            for a in range(3)
        )
        total = step_columns(total, 1 - b, breadth)
        out[...] = total if b == 1 else out[...] + total


def upstream_back(own, low, high, kernel, breadth):
    cells, width = own.shape
    return call(
        functools.partial(upstream_body, breadth),
        (own, low, high, kernel),
        [((cells + 2 * breadth, kernel.shape[2]), WIDE)],
        2 * cells * kernel.size,
        [pltpu.VMEM((cells + 2 * low.shape[0], width), NARROW)],
    )[0]


def head_body(
    breadth, info, low, top, inner, bottom, high, kernel, grad_hidden, hidden, own_pre, field, grad, padded, grad_pre
):
    cells = grad.shape[0]
    tall = hidden.shape[0]
    at = 0
    for part in (low, top, inner, bottom, high):
        padded[at : at + part.shape[0]] = part[...]
        at += part.shape[0]
    field[...] = padded[breadth : breadth + tall]
    pre = sum(
        step_columns(
            sum(matmul(padded[a * breadth : a * breadth + tall], kernel[a, b]) for a in range(3)),
            b - 1,
            breadth,
        )
        for b in (1, 0, 2)
    )
    row = lax.broadcasted_iota(jnp.int32, pre.shape, 0)
    inside = ((row >= breadth) | (info[4] > 0)) & ((row < tall - breadth) | (info[5] > 0))
    sigma = 1.0 / (1.0 + jnp.exp(-pre))
    hidden[...] = jnp.where(inside, pre * sigma, 0.0).astype(NARROW)
    slope = grad_hidden[...] * (sigma * (1.0 + pre * (1.0 - sigma)))
    grad_pre[...] = jnp.where(inside, slope, 0.0).astype(NARROW)
    own_pre[...] = grad_pre[breadth : breadth + cells]
    total = sum(
        step_columns(
            sum(
                matmul_turned(
                    grad_pre[(2 - a) * breadth : (2 - a) * breadth + cells], kernel[a, b]
                )
                for a in range(3)
            ),
            1 - b,
            breadth,
        )
        for b in (1, 0, 2)
    )
    grad[...] = total.astype(NARROW)


def head(info, parts, kernel, grad_hidden, breadth):
    inputs = parts[0].shape[1]
    tall, width = grad_hidden.shape
    cells = tall - 2 * breadth
    return call(
        functools.partial(head_body, breadth),
        (info, *parts, kernel, grad_hidden),
        [((tall, width), NARROW), ((cells, width), NARROW), ((tall, inputs), NARROW), ((cells, inputs), NARROW)],
        4 * cells * kernel.size,
        [pltpu.VMEM((tall + 2 * breadth, inputs), NARROW), pltpu.VMEM((tall, width), NARROW)],
        spaces=(pltpu.SMEM,) + (pltpu.VMEM,) * 7,
    )


def decode_body(breadth, hidden, kernel, out):
    cells = out.shape[0]
    total = sum(
        step_columns(
            sum(matmul(hidden[a * breadth : a * breadth + cells], kernel[a, b]) for a in range(3)),
            b - 1,
            breadth,
        )
        for b in (1, 0, 2)
    )
    out[...] = total.astype(NARROW)


def decode(hidden, kernel, breadth):
    tall = hidden.shape[0]
    return call(
        functools.partial(decode_body, breadth),
        (hidden, kernel),
        [((tall - 2 * breadth, kernel.shape[3]), NARROW)],
        2 * (tall - 2 * breadth) * kernel.size,
    )[0]


def term_of(info, place, weights, field):
    cells = field.shape[0]
    rows = pl.ds(pl.multiple_of(info[place] * cells, cells), cells)
    return lax.dot_general(
        weights[rows, :], field[...], (((0,), (0,)), ((), ())), preferred_element_type=WIDE
    )


def book_start_body(info, weights, own, beside, across, out):
    out[...] = term_of(info, 3, weights, own)
    out[...] += term_of(info, 2, weights, beside)
    out[...] += term_of(info, 1, weights, across)


def book_end_body(info, weights, corner, base, mine, other, total):
    total[...] = base[...] + term_of(info, 0, weights, corner)
    half = mine.shape[0]
    core = info[6]
    mine[...] = total[pl.ds(pl.multiple_of(core * half, half), half), :].astype(NARROW)
    other[...] = total[pl.ds(pl.multiple_of((1 - core) * half, half), half), :].astype(NARROW)


def book_start(info, weights, own, beside, across):
    shape = (weights.shape[1], own.shape[1])
    return call(
        book_start_body,
        (info, weights, own, beside, across),
        [(shape, WIDE)],
        6 * weights.shape[1] * own.size,
        spaces=(pltpu.SMEM,) + (pltpu.VMEM,) * 4,
    )[0]


def book_end(info, weights, corner, base):
    half = (base.shape[0] // 2, base.shape[1])
    return (
        book_end_body,
        (info, weights, corner, base),
        [(half, NARROW), (half, NARROW)],
        [pltpu.VMEM(base.shape, WIDE)],
    )


def halves_body(mine, got, first, second):
    half = first.shape[0]
    first[...] = plus(mine[:half], got[:half])
    second[...] = plus(mine[half:], got[half:])


def halves(mine, got):
    half = (mine.shape[0] // 2, mine.shape[1])
    return halves_body, (mine, got), [(half, NARROW), (half, NARROW)], []


def pair_body(first, got_first, second, got_second, *outs):
    half = first.shape[0]
    if len(outs) == 2:
        outs[0][...] = plus(first[...], got_first[...])
        outs[1][...] = plus(second[...], got_second[...])
    else:
        outs[0][:half] = plus(first[...], got_first[...])
        outs[0][half:] = plus(second[...], got_second[...])


def pair(first, got_first, second, got_second, joined):
    rows, lanes = first.shape
    outs = [((2 * rows, lanes), NARROW)] if joined else [((rows, lanes), NARROW)] * 2
    return pair_body, (first, got_first, second, got_second), outs, []


def kernel_grad_part(breadth, at, pick, own_up, far_up, own_field, far_field, outs, turned):
    keep_a, send_a, keep_b, send_b = outs
    cells = own_up.shape[0]
    half = pick.shape[0]
    lanes = own_field.shape[1] // 2
    parts = send_a.shape[0] + 1
    tall = half // parts
    short = tall // 2
    for source, ref in enumerate((own_up, far_up)):
        across = matmul_turned(pick[...], ref[...])
        column = lax.broadcasted_iota(jnp.int32, across.shape, 1) % breadth
        later = jnp.where(column == breadth - 1, 0.0, pltpu.roll(across, cells - 1, 1))
        sooner = jnp.where(column == 0, 0.0, pltpu.roll(across, 1, 1))
        for b, value in enumerate((later, across, sooner)):
            turned[source, b * half : (b + 1) * half, :] = value.astype(NARROW)

    @pl.loop(0, 3)
    def _(a):
        rows = pl.ds(pl.multiple_of(a * breadth, breadth), cells)
        total = matmul(turned[0], own_field[rows, :]) + matmul(turned[1], far_field[rows, :])
        total = total.astype(NARROW)
        for b in range(3):
            for k in range(parts):
                base = b * half + k * tall
                block = total[base : base + tall]
                if k == 0:
                    keep_a[a, b, :, at : at + lanes] = block[:, :lanes]
                else:
                    send_a[k - 1, a, b, :, at : at + lanes] = block[:, :lanes]
                keep_b[a, b, k, :, at : at + lanes] = block[:short, lanes:]
                send_b[a, b, k, :, at : at + lanes] = block[short:, lanes:]


def kernel_grads_body(breadth, pick, *refs):
    outs, turned = refs[8:12], refs[-1]
    kernel_grad_part(breadth, 0, pick, *refs[:4], outs, turned)
    kernel_grad_part(breadth, refs[2].shape[1] // 2, pick, *refs[4:8], outs, turned)


def kernel_grads(pick, two, one, breadth, parts):
    half = pick.shape[0]
    cells = two[0].shape[0]
    tall = half // parts
    lanes = (two[2].shape[1] + one[2].shape[1]) // 2
    shapes = [
        (3, 3, tall, lanes),
        (parts - 1, 3, 3, tall, lanes),
        (3, 3, parts, tall // 2, lanes),
        (3, 3, parts, tall // 2, lanes),
    ]
    return call(
        functools.partial(kernel_grads_body, breadth),
        (pick, *two, *one),
        [(shape, NARROW) for shape in shapes],
        36 * half * (two[2].size + one[2].size),
        [pltpu.VMEM((2, 3 * half, cells), NARROW)],
        limit=LARGE,
    )


def own_channels(width):
    parts = lax.axis_size("space") // 2
    space = lax.axis_index("space")
    code = lax.axis_index("code")
    clip = lax.axis_index("clip")
    grain = width // (parts * 16)
    index = jnp.arange(width // 2)
    inner = index % grain
    d_code = (index // grain) % 4
    d_clip = (index // (grain * 4)) % 2
    d_space = index // (grain * 8)
    owner = ((space ^ (2 * d_space)) * 4 + (code ^ d_code)) * 2 + (clip ^ d_clip)
    channel = owner * grain + inner
    return (channel[:, None] == jnp.arange(width)[None, :]).astype(NARROW)


def turn_body(keep_a, keep_b, got_b, *refs):
    keep_first, send_first, keep_second, send_second = refs[-4:]
    got_a = refs[:-4]
    short = keep_first.shape[2]
    for a in range(3):
        for b in range(3):
            total = plus(keep_a[a, b], *[got[a, b] for got in got_a])
            keep_first[a, b] = total[:short]
            send_first[a, b] = total[short:]
            total = plus(keep_b[a, b], got_b[a, b])
            keep_second[a, b] = total[0]
            for k in range(1, total.shape[0]):
                send_second[k - 1, a, b] = total[k]


def along_body(keep_first, got_first, keep_second, *refs):
    outs = refs[-4:] if refs[-1].shape[2] * 4 == keep_first.shape[2] else refs[-1:]
    got_second = refs[: -len(outs)]
    lanes = keep_first.shape[3]
    grain = keep_first.shape[2] // len(outs)
    for a in range(3):
        for b in range(3):
            first = plus(keep_first[a, b], got_first[a, b])
            second = plus(keep_second[a, b], *[got[a, b] for got in got_second])
            for k, out in enumerate(outs):
                out[a, b, :, :lanes] = first[k * grain : (k + 1) * grain]
                out[a, b, :, lanes:] = second[k * grain : (k + 1) * grain]


class Spread:
    def __init__(self, parts_of, name):
        self.keep_a, send_a, self.keep_b, send_b = parts_of
        self.name = name
        self.parts = send_a.shape[0] + 1
        self.got_a = [swap(send_a[k - 1], "space", 2 * k, name + "_a1") for k in range(1, self.parts)]
        self.got_b = swap(send_b, "clip", 1, name + "_b1")

    def turn(self):
        tall, lanes = self.keep_a.shape[2:]
        shape = (3, 3, tall // 2, lanes)
        outs = [(shape, NARROW)] * 3 + [((self.parts - 1,) + shape, NARROW)]
        return turn_body, (self.keep_a, self.keep_b, self.got_b, *self.got_a), outs, []

    def turned(self, outs):
        self.first, send_first, self.second, send_second = outs
        self.got_a = swap(send_first, "clip", 1, self.name + "_a2")
        self.got_b = [
            swap(send_second[k - 1], "space", 2 * k, self.name + "_b2") for k in range(1, self.parts)
        ]

    def along(self):
        rows, lanes = self.first.shape[2:]
        outs = [((3, 3, rows, 2 * lanes), NARROW)]
        if rows % 64 == 0:
            outs = [((3, 3, rows // 4, 2 * lanes), NARROW)] * 4
        return along_body, (self.first, self.got_a, self.second, *self.got_b), outs, []

    def sent(self, outs):
        if len(outs) == 1:
            grain = outs[0].shape[2] // 4
            outs = [outs[0][:, :, k * grain : (k + 1) * grain] for k in range(4)]
        self.last = outs[0]
        self.got = [swap(outs[k], "code", k, self.name + "_z") for k in (2, 1, 3)]

    def done(self, split):
        total = sum(got.astype(WIDE) for got in self.got) + self.last.astype(WIDE)
        total = total.transpose(0, 1, 3, 2)
        half = total.shape[2] // 2
        one = jnp.concatenate([total[:, :, split:half], total[:, :, half + split :]], axis=2)
        two = jnp.concatenate([total[:, :, :split], total[:, :, half : half + split]], axis=2)
        return one, two


def on_device(soft_weights, codebook, kernel_one, kernel_two, cotangent):
    weights = soft_weights[0]
    weights = weights.reshape(-1, weights.shape[2])
    own_rows, breadth, width = cotangent.shape[1:]
    upstream = cotangent[0]
    cells = own_rows * breadth
    own_up = upstream.reshape(cells, width)
    parts = lax.axis_size("space") // 2
    code = lax.axis_index("code")
    space = lax.axis_index("space")
    place = space * 4 + code
    last = lax.axis_size("space") * 4 - 1
    flat = lambda field: field.reshape(-1, field.shape[2])
    info = jnp.stack([code ^ 3, code ^ 2, code ^ 1, code, place, last - place, space % 2, 0])
    info = info.astype(jnp.int32)

    edge = 2 * breadth
    (third,) = lookup((0,), info, weights, codebook, cells, edge, 2)
    from_pair = swap(third, "code", 1, "look_z1")
    upstream = after(own_up, third)
    cot_low, cot_high = edges(upstream[:edge], upstream[-edge:], "cot_edge")
    shards = lookup((1, 2, 3), info, weights, after(codebook, third), cells, edge, 1)
    pick = after(own_channels(width), shards[0])
    (second_ends, second, beside_ends, beside, own_ends, own), pick, cot_low, cot_high = (
        lax.optimization_barrier((shards, pick, cot_low, cot_high))
    )
    middle_ends = plus(second_ends, from_pair[: 2 * edge])
    far_ends = swap(middle_ends, "code", 2, "look_ends")
    near_ends = swap(beside_ends, "code", 1, "look_near_ends")
    middle = plus(after(second, middle_ends), from_pair[2 * edge :])
    far = swap(middle, "code", 2, "look_z2")
    near = swap(after(beside, middle), "code", 1, "look_near")
    grad_hidden = upstream_back(after(own_up, middle), cot_low, cot_high, kernel_two, breadth)
    far_up = swap(after(own_up, middle), "space", 1, "cot_core")
    own_ends, own, grad_hidden, far_up = lax.optimization_barrier(
        (own_ends, own, grad_hidden, far_up)
    )
    part = lambda k: slice(k * edge, (k + 1) * edge)
    top, bottom = [
        plus(own_ends[part(k)], near_ends[part(k)], far_ends[part(k)]) for k in range(2)
    ]
    low, high = edges(top, bottom, "embed_edge")
    inner = plus(after(own, top, bottom), near, far)
    hidden, own_pre, field, grad_embedded = head(
        info, (low, top, inner, bottom, high), kernel_one, grad_hidden, breadth
    )

    across = swap(grad_embedded, "code", 2, "ge_z2")
    beside = swap(grad_embedded, "code", 1, "ge_z1")
    far_hidden = swap(hidden, "space", 1, "hidden_core")
    far_pre = swap(own_pre, "space", 1, "pre_core")
    far_field = swap(field, "space", 1, "field_core")
    grads = kernel_grads(
        pick,
        (own_up, far_up, hidden, far_hidden),
        (own_pre, far_pre, field, far_field),
        breadth,
        parts,
    )
    across, beside = after((across, beside), grads[0])
    grads = Spread(grads, "grads")
    corner = swap(across, "code", 1, "ge_z3")
    term = book_start(info, weights, grad_embedded, beside, across)
    ((mine, other),) = fuse(book_end(info, weights, corner, term))
    got = swap(other, "space", 1, "book_core")
    ((first, second),) = fuse(halves(mine, got))

    stages = []
    bits = 2
    while bits < lax.axis_size("space"):
        stages.append(("space", bits))
        bits *= 2
    ways = list(zip(stages + [("clip", 1)], [("clip", 1)] + stages))
    for k, (way, back) in enumerate(ways):
        got_first, got_second = swap(first, *way, "book_a"), swap(second, *back, "book_b")
        if k == 0:
            (outs,) = fuse(grads.turn())
            grads.turned(outs)
            (outs,) = fuse(grads.along())
            grads.sent(outs)
            first = after(first, grads.last)
        elif k == len(ways) - 1:
            decoded = decode(after(hidden, first, second), kernel_two, breadth)
            first = after(first, decoded)
        (outs,) = fuse(pair(first, got_first, second, got_second, k == len(ways) - 1))
        if k < len(ways) - 1:
            first, second = outs
    (mine,) = outs
    other = swap(mine, "space", 1, "book_back")
    core = space % 2
    low = jnp.where(core == 0, mine, other)
    high = jnp.where(core == 0, other, mine)
    grad_codebook = jnp.concatenate([low, high], axis=0).astype(WIDE)
    grad_one, grad_two = grads.done(width // 2)
    return (decoded.reshape(cotangent.shape), grad_one, grad_two, grad_codebook)


def solution(mesh):
    in_specs = (
        P("clip", "space", None, "code"),
        P("code", None),
        P(),
        P(),
        P("clip", ("space", "code"), None, None),
    )
    out_specs = (
        P("clip", ("space", "code"), None, None),
        P(None, None, None, ("space", "code", "clip")),
        P(None, None, None, ("space", "code", "clip")),
        P("code", None),
    )
    return jax.shard_map(
        on_device, mesh=mesh, in_specs=in_specs, out_specs=out_specs, check_vma=False
    )
```

```python
import functools

import jax
import jax.numpy as jnp
from jax import lax
from jax.experimental import pallas as pl
from jax.experimental.pallas import tpu as pltpu
from jax.sharding import PartitionSpec as P

NARROW = jnp.bfloat16
WIDE = jnp.float32
COST = 8
SMALL, LARGE, WHOLE = 16 * 1024 * 1024, 24 * 1024 * 1024, 56 * 1024 * 1024


def swap(value, axis, bits, name):
    with jax.named_scope(name):
        return lax.ppermute(value, axis, [(i, i ^ bits) for i in range(lax.axis_size(axis))])


def after(value, *others):
    return lax.optimization_barrier((value, *others))[0]


def plus(*terms):
    return sum(term.astype(WIDE) for term in terms).astype(NARROW)


def edges(top, bottom, name):
    axes = ("space", "code")
    count = lax.axis_size(axes)
    forward = [(i, i + 1) for i in range(count - 1)]
    backward = [(i + 1, i) for i in range(count - 1)]
    with jax.named_scope(name):
        low = lax.ppermute(bottom, axes, forward)
        high = lax.ppermute(top, axes, backward)
    return low, high


def matmul(left, right):
    return jnp.dot(left, right, preferred_element_type=WIDE)


def matmul_turned(left, right):
    return lax.dot_general(left, right, (((1,), (1,)), ((), ())), preferred_element_type=WIDE)


def step_columns(value, offset, breadth):
    if offset == 0:
        return value
    count = value.shape[0]
    column = lax.broadcasted_iota(jnp.int32, value.shape, 0) % breadth
    moved = pltpu.roll(value, (-offset) % count, 0)
    return jnp.where(column == (0 if offset < 0 else breadth - 1), 0.0, moved)


def call(body, operands, outs, flops, scratch=(), limit=SMALL, spaces=None):
    local = pl.BlockSpec(memory_space=pltpu.VMEM)
    return pl.pallas_call(
        body,
        in_specs=[pl.BlockSpec(memory_space=space) for space in spaces] if spaces else [local] * len(operands),
        out_specs=[local] * len(outs),
        out_shape=[jax.ShapeDtypeStruct(shape, dtype) for shape, dtype in outs],
        scratch_shapes=list(scratch),
        compiler_params=pltpu.CompilerParams(vmem_limit_bytes=limit),
        cost_estimate=pl.CostEstimate(flops=flops // COST, bytes_accessed=1, transcendentals=0),
    )(*operands)


def fuse(*tasks):
    spans = [(len(operands), len(outs), len(scratch)) for _, operands, outs, scratch in tasks]
    counts = [sum(span[k] for span in spans) for k in range(3)]

    def body(*refs):
        at = [0, counts[0], counts[0] + counts[1]]
        for (task, *_), span in zip(tasks, spans):
            picked = []
            for k in range(3):
                picked += refs[at[k] : at[k] + span[k]]
                at[k] += span[k]
            task(*picked)

    operands = [operand for task in tasks for operand in task[1]]
    results = list(
        call(
            body,
            operands,
            [out for task in tasks for out in task[2]],
            8 * 10**8,
            [item for task in tasks for item in task[3]],
            spaces=[pltpu.SMEM if item.dtype == jnp.int32 else pltpu.VMEM for item in operands],
        )
    )
    return [[results.pop(0) for _ in range(span[1])] for span in spans]


def lookup_body(count, edge, order, weights, codebook, *refs):
    outs, total = refs[:-1], refs[-1]
    shard, step = pl.program_id(0), pl.program_id(1)
    last = pl.num_programs(1) - 1
    term = matmul(weights[...], codebook[...])

    @pl.when(step == 0)
    def _():
        total[...] = term

    @pl.when(step > 0)
    def _():
        total[...] += term

    for k in range(count):

        @pl.when((step == last) & (shard == k))
        def _():
            if len(outs) == count:
                ends, inner = outs[k].at[: 2 * edge], outs[k].at[2 * edge :]
            elif k == 0:
                ends, inner = outs[0].at[: 2 * edge], outs[0].at[2 * edge :]
            else:
                ends, inner = outs[2 * k - 1], outs[2 * k]
            ends[:edge] = total[:edge].astype(NARROW)
            ends[edge:] = total[-edge:].astype(NARROW)
            inner[...] = total[edge:-edge].astype(NARROW)


def lookup(places, info, weights, codebook, cells, edge, split):
    codes, inner = codebook.shape
    count = len(places)
    first = places[0]
    rows = [cells] + [2 * edge, cells - 2 * edge] * (count - 1)
    return pl.pallas_call(
        functools.partial(lookup_body, count, edge),
        grid_spec=pltpu.PrefetchScalarGridSpec(
            num_scalar_prefetch=1,
            grid=(count, split),
            in_specs=[
                pl.BlockSpec((cells, codes // split), lambda i, j, order: (order[first + i], j)),
                pl.BlockSpec((codes // split, inner), lambda i, j, order: (j, 0)),
            ],
            out_specs=[pl.BlockSpec((height, inner), lambda i, j, order: (0, 0)) for height in rows],
            scratch_shapes=[pltpu.VMEM((cells, inner), WIDE)],
        ),
        out_shape=[jax.ShapeDtypeStruct((height, inner), NARROW) for height in rows],
        compiler_params=pltpu.CompilerParams(vmem_limit_bytes=WHOLE),
        cost_estimate=pl.CostEstimate(
            flops=2 * count * cells * codebook.size // COST, bytes_accessed=1, transcendentals=0
        ),
    )(info, weights, codebook)


def upstream_body(breadth, own, low, high, kernel, out, padded):
    edge = low.shape[0]
    cells = own.shape[0]
    tall = out.shape[0]
    padded[:edge] = low[...]
    padded[edge : edge + cells] = own[...]
    padded[edge + cells :] = high[...]
    for b in (1, 0, 2):
        total = sum(
            matmul_turned(padded[(2 - a) * breadth : (2 - a) * breadth + tall], kernel[a, b])
            for a in range(3)
        )
        total = step_columns(total, 1 - b, breadth)
        out[...] = total if b == 1 else out[...] + total


def upstream_back(own, low, high, kernel, breadth):
    cells, width = own.shape
    return call(
        functools.partial(upstream_body, breadth),
        (own, low, high, kernel),
        [((cells + 2 * breadth, kernel.shape[2]), WIDE)],
        2 * cells * kernel.size,
        [pltpu.VMEM((cells + 2 * low.shape[0], width), NARROW)],
    )[0]


def head_body(
    breadth, info, low, top, inner, bottom, high, kernel, grad_hidden, hidden, own_pre, field, grad, padded, grad_pre
):
    cells = grad.shape[0]
    tall = hidden.shape[0]
    at = 0
    for part in (low, top, inner, bottom, high):
        padded[at : at + part.shape[0]] = part[...]
        at += part.shape[0]
    field[...] = padded[breadth : breadth + tall]
    pre = sum(
        step_columns(
            sum(matmul(padded[a * breadth : a * breadth + tall], kernel[a, b]) for a in range(3)),
            b - 1,
            breadth,
        )
        for b in (1, 0, 2)
    )
    row = lax.broadcasted_iota(jnp.int32, pre.shape, 0)
    inside = ((row >= breadth) | (info[7] > 0)) & ((row < tall - breadth) | (info[8] > 0))
    sigma = 1.0 / (1.0 + jnp.exp(-pre))
    hidden[...] = jnp.where(inside, pre * sigma, 0.0).astype(NARROW)
    slope = grad_hidden[...] * (sigma * (1.0 + pre * (1.0 - sigma)))
    grad_pre[...] = jnp.where(inside, slope, 0.0).astype(NARROW)
    own_pre[...] = grad_pre[breadth : breadth + cells]
    total = sum(
        step_columns(
            sum(
                matmul_turned(
                    grad_pre[(2 - a) * breadth : (2 - a) * breadth + cells], kernel[a, b]
                )
                for a in range(3)
            ),
            1 - b,
            breadth,
        )
        for b in (1, 0, 2)
    )
    grad[...] = total.astype(NARROW)


def head(info, parts, kernel, grad_hidden, breadth):
    inputs = parts[0].shape[1]
    tall, width = grad_hidden.shape
    cells = tall - 2 * breadth
    return call(
        functools.partial(head_body, breadth),
        (info, *parts, kernel, grad_hidden),
        [((tall, width), NARROW), ((cells, width), NARROW), ((tall, inputs), NARROW), ((cells, inputs), NARROW)],
        4 * cells * kernel.size,
        [pltpu.VMEM((tall + 2 * breadth, inputs), NARROW), pltpu.VMEM((tall, width), NARROW)],
        spaces=(pltpu.SMEM,) + (pltpu.VMEM,) * 7,
    )


def decode_body(breadth, hidden, kernel, out):
    cells = out.shape[0]
    total = sum(
        step_columns(
            sum(matmul(hidden[a * breadth : a * breadth + cells], kernel[a, b]) for a in range(3)),
            b - 1,
            breadth,
        )
        for b in (1, 0, 2)
    )
    out[...] = total.astype(NARROW)


def decode(hidden, kernel, breadth):
    tall = hidden.shape[0]
    return call(
        functools.partial(decode_body, breadth),
        (hidden, kernel),
        [((tall - 2 * breadth, kernel.shape[3]), NARROW)],
        2 * (tall - 2 * breadth) * kernel.size,
    )[0]


def term_of(info, place, weights, field):
    cells = field.shape[0]
    rows = pl.ds(pl.multiple_of(info[place] * cells, cells), cells)
    return lax.dot_general(
        weights[rows, :], field[...], (((0,), (0,)), ((), ())), preferred_element_type=WIDE
    )


def book_start_body(info, weights, own, beside, across, out):
    out[...] = term_of(info, 3, weights, own)
    out[...] += term_of(info, 2, weights, beside)
    out[...] += term_of(info, 1, weights, across)


def book_end_body(info, weights, corner, base, mine, other, total):
    total[...] = base[...] + term_of(info, 0, weights, corner)
    half = mine.shape[0]
    core = info[9]
    mine[...] = total[pl.ds(pl.multiple_of(core * half, half), half), :].astype(NARROW)
    other[...] = total[pl.ds(pl.multiple_of((1 - core) * half, half), half), :].astype(NARROW)


def book_start(info, weights, own, beside, across):
    shape = (weights.shape[1], own.shape[1])
    return call(
        book_start_body,
        (info, weights, own, beside, across),
        [(shape, WIDE)],
        6 * weights.shape[1] * own.size,
        spaces=(pltpu.SMEM,) + (pltpu.VMEM,) * 4,
    )[0]


def book_end(info, weights, corner, base):
    half = (base.shape[0] // 2, base.shape[1])
    return (
        book_end_body,
        (info, weights, corner, base),
        [(half, NARROW), (half, NARROW)],
        [pltpu.VMEM(base.shape, WIDE)],
    )


def halves_body(mine, got, first, second):
    half = first.shape[0]
    first[...] = plus(mine[:half], got[:half])
    second[...] = plus(mine[half:], got[half:])


def halves(mine, got):
    half = (mine.shape[0] // 2, mine.shape[1])
    return halves_body, (mine, got), [(half, NARROW), (half, NARROW)], []


def pair_body(first, got_first, second, got_second, *outs):
    half = first.shape[0]
    if len(outs) == 2:
        outs[0][...] = plus(first[...], got_first[...])
        outs[1][...] = plus(second[...], got_second[...])
    else:
        outs[0][:half] = plus(first[...], got_first[...])
        outs[0][half:] = plus(second[...], got_second[...])


def pair(first, got_first, second, got_second, joined):
    rows, lanes = first.shape
    outs = [((2 * rows, lanes), NARROW)] if joined else [((rows, lanes), NARROW)] * 2
    return pair_body, (first, got_first, second, got_second), outs, []


def kernel_grad_part(breadth, at, pick, own_up, far_up, own_field, far_field, outs, turned):
    keep_a, send_a, keep_b, send_b = outs
    cells = own_up.shape[0]
    half = pick.shape[0]
    lanes = own_field.shape[1] // 2
    parts = send_a.shape[0] + 1
    tall = half // parts
    short = tall // 2
    for source, ref in enumerate((own_up, far_up)):
        across = matmul_turned(pick[...], ref[...])
        column = lax.broadcasted_iota(jnp.int32, across.shape, 1) % breadth
        later = jnp.where(column == breadth - 1, 0.0, pltpu.roll(across, cells - 1, 1))
        sooner = jnp.where(column == 0, 0.0, pltpu.roll(across, 1, 1))
        for b, value in enumerate((later, across, sooner)):
            turned[source, b * half : (b + 1) * half, :] = value.astype(NARROW)

    @pl.loop(0, 3)
    def _(a):
        rows = pl.ds(pl.multiple_of(a * breadth, breadth), cells)
        total = matmul(turned[0], own_field[rows, :]) + matmul(turned[1], far_field[rows, :])
        total = total.astype(NARROW)
        for b in range(3):
            for k in range(parts):
                base = b * half + k * tall
                block = total[base : base + tall]
                if k == 0:
                    keep_a[a, b, :, at : at + lanes] = block[:, :lanes]
                else:
                    send_a[k - 1, a, b, :, at : at + lanes] = block[:, :lanes]
                keep_b[a, b, k, :, at : at + lanes] = block[:short, lanes:]
                send_b[a, b, k, :, at : at + lanes] = block[short:, lanes:]


def kernel_grads_body(breadth, pick, *refs):
    outs, turned = refs[8:12], refs[-1]
    kernel_grad_part(breadth, 0, pick, *refs[:4], outs, turned)
    kernel_grad_part(breadth, refs[2].shape[1] // 2, pick, *refs[4:8], outs, turned)


def kernel_grads(pick, two, one, breadth, parts):
    half = pick.shape[0]
    cells = two[0].shape[0]
    tall = half // parts
    lanes = (two[2].shape[1] + one[2].shape[1]) // 2
    shapes = [
        (3, 3, tall, lanes),
        (parts - 1, 3, 3, tall, lanes),
        (3, 3, parts, tall // 2, lanes),
        (3, 3, parts, tall // 2, lanes),
    ]
    return call(
        functools.partial(kernel_grads_body, breadth),
        (pick, *two, *one),
        [(shape, NARROW) for shape in shapes],
        36 * half * (two[2].size + one[2].size),
        [pltpu.VMEM((2, 3 * half, cells), NARROW)],
        limit=LARGE,
    )


def own_channels(width):
    parts = lax.axis_size("space") // 2
    space = lax.axis_index("space")
    code = lax.axis_index("code")
    clip = lax.axis_index("clip")
    grain = width // (parts * 16)
    index = jnp.arange(width // 2)
    inner = index % grain
    d_code = (index // grain) % 4
    d_clip = (index // (grain * 4)) % 2
    d_space = index // (grain * 8)
    owner = ((space ^ (2 * d_space)) * 4 + (code ^ d_code)) * 2 + (clip ^ d_clip)
    channel = owner * grain + inner
    return (channel[:, None] == jnp.arange(width)[None, :]).astype(NARROW)


def turn_body(keep_a, keep_b, got_b, *refs):
    keep_first, send_first, keep_second, send_second = refs[-4:]
    got_a = refs[:-4]
    short = keep_first.shape[2]
    for a in range(3):
        for b in range(3):
            total = plus(keep_a[a, b], *[got[a, b] for got in got_a])
            keep_first[a, b] = total[:short]
            send_first[a, b] = total[short:]
            total = plus(keep_b[a, b], got_b[a, b])
            keep_second[a, b] = total[0]
            for k in range(1, total.shape[0]):
                send_second[k - 1, a, b] = total[k]


def along_body(keep_first, got_first, keep_second, *refs):
    outs = refs[-4:] if refs[-1].shape[2] * 4 == keep_first.shape[2] else refs[-1:]
    got_second = refs[: -len(outs)]
    lanes = keep_first.shape[3]
    grain = keep_first.shape[2] // len(outs)
    for a in range(3):
        for b in range(3):
            first = plus(keep_first[a, b], got_first[a, b])
            second = plus(keep_second[a, b], *[got[a, b] for got in got_second])
            for k, out in enumerate(outs):
                out[a, b, :, :lanes] = first[k * grain : (k + 1) * grain]
                out[a, b, :, lanes:] = second[k * grain : (k + 1) * grain]


class Spread:
    def __init__(self, parts_of, name):
        self.keep_a, send_a, self.keep_b, send_b = parts_of
        self.name = name
        self.parts = send_a.shape[0] + 1
        self.got_a = [swap(send_a[k - 1], "space", 2 * k, name + "_a1") for k in range(1, self.parts)]
        self.got_b = swap(send_b, "clip", 1, name + "_b1")

    def turn(self):
        tall, lanes = self.keep_a.shape[2:]
        shape = (3, 3, tall // 2, lanes)
        outs = [(shape, NARROW)] * 3 + [((self.parts - 1,) + shape, NARROW)]
        return turn_body, (self.keep_a, self.keep_b, self.got_b, *self.got_a), outs, []

    def turned(self, outs):
        self.first, send_first, self.second, send_second = outs
        self.got_a = swap(send_first, "clip", 1, self.name + "_a2")
        self.got_b = [
            swap(send_second[k - 1], "space", 2 * k, self.name + "_b2") for k in range(1, self.parts)
        ]

    def along(self):
        rows, lanes = self.first.shape[2:]
        outs = [((3, 3, rows, 2 * lanes), NARROW)]
        if rows % 64 == 0:
            outs = [((3, 3, rows // 4, 2 * lanes), NARROW)] * 4
        return along_body, (self.first, self.got_a, self.second, *self.got_b), outs, []

    def sent(self, outs):
        if len(outs) == 1:
            grain = outs[0].shape[2] // 4
            outs = [outs[0][:, :, k * grain : (k + 1) * grain] for k in range(4)]
        self.last = outs[0]
        self.got = [swap(outs[k], "code", k, self.name + "_z") for k in (2, 1, 3)]

    def done(self, split):
        total = sum(got.astype(WIDE) for got in self.got) + self.last.astype(WIDE)
        total = total.transpose(0, 1, 3, 2)
        half = total.shape[2] // 2
        one = jnp.concatenate([total[:, :, split:half], total[:, :, half + split :]], axis=2)
        two = jnp.concatenate([total[:, :, :split], total[:, :, half : half + split]], axis=2)
        return one, two


def on_device(soft_weights, codebook, kernel_one, kernel_two, cotangent):
    weights = soft_weights[0]
    weights = weights.reshape(-1, weights.shape[2])
    own_rows, breadth, width = cotangent.shape[1:]
    upstream = cotangent[0]
    cells = own_rows * breadth
    own_up = upstream.reshape(cells, width)
    parts = lax.axis_size("space") // 2
    code = lax.axis_index("code")
    space = lax.axis_index("space")
    place = space * 4 + code
    last = lax.axis_size("space") * 4 - 1
    flat = lambda field: field.reshape(-1, field.shape[2])
    info = jnp.stack(
        [code ^ 3, code ^ 2, code ^ 1, code, code ^ 1, code ^ 2, code, place, last - place, space % 2]
    )
    info = info.astype(jnp.int32)

    edge = 2 * breadth
    (third,) = lookup((0,), info, weights, codebook, cells, edge, 2)
    from_pair = swap(third, "code", 1, "look_z1")
    shards = lookup((4, 5, 6), info, weights, after(codebook, third), cells, edge, 1)
    pick = after(own_channels(width), shards[0])
    (beside, second_ends, second, own_ends, own), pick = lax.optimization_barrier(
        (shards, pick)
    )
    middle_ends = plus(second_ends, from_pair[: 2 * edge])
    far_ends = swap(middle_ends, "code", 2, "look_ends")
    near = swap(beside, "code", 1, "look_near")
    middle = plus(after(second, middle_ends), from_pair[2 * edge :])
    far = swap(middle, "code", 2, "look_z2")
    upstream = after(own_up, middle)
    cot_low, cot_high = edges(upstream[:edge], upstream[-edge:], "cot_edge")
    part = lambda k: slice(k * edge, (k + 1) * edge)
    top, bottom = [
        plus(own_ends[part(k)], near[part(k)], far_ends[part(k)]) for k in range(2)
    ]
    low, high = edges(top, bottom, "embed_edge")
    upstream = after(own_up, top, bottom)
    far_up = swap(after(own_up, top), "space", 1, "cot_core")
    grad_hidden = upstream_back(upstream, cot_low, cot_high, kernel_two, breadth)
    inner = plus(after(own, top, bottom), near[2 * edge :], far)
    hidden, own_pre, field, grad_embedded = head(
        info, (low, top, inner, bottom, high), kernel_one, grad_hidden, breadth
    )

    across = swap(grad_embedded, "code", 2, "ge_z2")
    beside = swap(grad_embedded, "code", 1, "ge_z1")
    far_hidden = swap(hidden, "space", 1, "hidden_core")
    far_pre = swap(own_pre, "space", 1, "pre_core")
    far_field = swap(field, "space", 1, "field_core")
    grads = kernel_grads(
        pick,
        (own_up, far_up, hidden, far_hidden),
        (own_pre, far_pre, field, far_field),
        breadth,
        parts,
    )
    across, beside = after((across, beside), grads[0])
    grads = Spread(grads, "grads")
    corner = swap(across, "code", 1, "ge_z3")
    term = book_start(info, weights, grad_embedded, beside, across)
    (outs,) = fuse(grads.turn())
    grads.turned(outs)
    ((mine, other),) = fuse(book_end(info, weights, corner, after(term, grads.first)))
    got = swap(other, "space", 1, "book_core")
    ((first, second),) = fuse(halves(mine, got))

    stages = []
    bits = 2
    while bits < lax.axis_size("space"):
        stages.append(("space", bits))
        bits *= 2
    ways = list(zip(stages + [("clip", 1)], [("clip", 1)] + stages))
    for k, (way, back) in enumerate(ways):
        got_first, got_second = swap(first, *way, "book_a"), swap(second, *back, "book_b")
        if k == 0:
            decoded = decode(after(hidden, first), kernel_two, breadth)
            grads.second = after(grads.second, decoded)
            (outs,) = fuse(grads.along())
            grads.sent(outs)
            first = after(first, grads.last)
        (outs,) = fuse(pair(first, got_first, second, got_second, k == len(ways) - 1))
        if k < len(ways) - 1:
            first, second = outs
    (mine,) = outs
    other = swap(mine, "space", 1, "book_back")
    core = space % 2
    low = jnp.where(core == 0, mine, other)
    high = jnp.where(core == 0, other, mine)
    grad_codebook = jnp.concatenate([low, high], axis=0).astype(WIDE)
    grad_one, grad_two = grads.done(width // 2)
    return (decoded.reshape(cotangent.shape), grad_one, grad_two, grad_codebook)


def solution(mesh):
    in_specs = (
        P("clip", "space", None, "code"),
        P("code", None),
        P(),
        P(),
        P("clip", ("space", "code"), None, None),
    )
    out_specs = (
        P("clip", ("space", "code"), None, None),
        P(None, None, None, ("space", "code", "clip")),
        P(None, None, None, ("space", "code", "clip")),
        P("code", None),
    )
    return jax.shard_map(
        on_device, mesh=mesh, in_specs=in_specs, out_specs=out_specs, check_vma=False
    )
```

```python
import functools

import jax
import jax.numpy as jnp
from jax import lax
from jax.experimental import pallas as pl
from jax.experimental.pallas import tpu as pltpu
from jax.sharding import PartitionSpec as P

NARROW = jnp.bfloat16
WIDE = jnp.float32
COST = 8
SMALL, LARGE, WHOLE = 16 * 1024 * 1024, 24 * 1024 * 1024, 56 * 1024 * 1024


def swap(value, axis, bits, name):
    with jax.named_scope(name):
        return lax.ppermute(value, axis, [(i, i ^ bits) for i in range(lax.axis_size(axis))])


def after(value, *others):
    return lax.optimization_barrier((value, *others))[0]


def plus(*terms):
    return sum(term.astype(WIDE) for term in terms).astype(NARROW)


def edges(top, bottom, name):
    axes = ("space", "code")
    count = lax.axis_size(axes)
    forward = [(i, i + 1) for i in range(count - 1)]
    backward = [(i + 1, i) for i in range(count - 1)]
    with jax.named_scope(name):
        low = lax.ppermute(bottom, axes, forward)
        high = lax.ppermute(top, axes, backward)
    return low, high


def matmul(left, right):
    return jnp.dot(left, right, preferred_element_type=WIDE)


def matmul_turned(left, right):
    return lax.dot_general(left, right, (((1,), (1,)), ((), ())), preferred_element_type=WIDE)


def step_columns(value, offset, breadth):
    if offset == 0:
        return value
    count = value.shape[0]
    column = lax.broadcasted_iota(jnp.int32, value.shape, 0) % breadth
    moved = pltpu.roll(value, (-offset) % count, 0)
    return jnp.where(column == (0 if offset < 0 else breadth - 1), 0.0, moved)


def call(body, operands, outs, flops, scratch=(), limit=SMALL, spaces=None):
    local = pl.BlockSpec(memory_space=pltpu.VMEM)
    return pl.pallas_call(
        body,
        in_specs=[pl.BlockSpec(memory_space=space) for space in spaces] if spaces else [local] * len(operands),
        out_specs=[local] * len(outs),
        out_shape=[jax.ShapeDtypeStruct(shape, dtype) for shape, dtype in outs],
        scratch_shapes=list(scratch),
        compiler_params=pltpu.CompilerParams(vmem_limit_bytes=limit),
        cost_estimate=pl.CostEstimate(flops=flops // COST, bytes_accessed=1, transcendentals=0),
    )(*operands)


def fuse(*tasks):
    spans = [(len(operands), len(outs), len(scratch)) for _, operands, outs, scratch in tasks]
    counts = [sum(span[k] for span in spans) for k in range(3)]

    def body(*refs):
        at = [0, counts[0], counts[0] + counts[1]]
        for (task, *_), span in zip(tasks, spans):
            picked = []
            for k in range(3):
                picked += refs[at[k] : at[k] + span[k]]
                at[k] += span[k]
            task(*picked)

    operands = [operand for task in tasks for operand in task[1]]
    results = list(
        call(
            body,
            operands,
            [out for task in tasks for out in task[2]],
            8 * 10**8,
            [item for task in tasks for item in task[3]],
            spaces=[pltpu.SMEM if item.dtype == jnp.int32 else pltpu.VMEM for item in operands],
        )
    )
    return [[results.pop(0) for _ in range(span[1])] for span in spans]


def lookup_body(count, edge, order, weights, codebook, *refs):
    outs, total = refs[:-1], refs[-1]
    shard, step = pl.program_id(0), pl.program_id(1)
    last = pl.num_programs(1) - 1
    term = matmul(weights[...], codebook[...])

    @pl.when(step == 0)
    def _():
        total[...] = term

    @pl.when(step > 0)
    def _():
        total[...] += term

    for k in range(count):

        @pl.when((step == last) & (shard == k))
        def _():
            if len(outs) == count:
                ends, inner = outs[k].at[: 2 * edge], outs[k].at[2 * edge :]
            elif k == 0:
                ends, inner = outs[0].at[: 2 * edge], outs[0].at[2 * edge :]
            else:
                ends, inner = outs[2 * k - 1], outs[2 * k]
            ends[:edge] = total[:edge].astype(NARROW)
            ends[edge:] = total[-edge:].astype(NARROW)
            inner[...] = total[edge:-edge].astype(NARROW)


def lookup(places, info, weights, codebook, cells, edge, split):
    codes, inner = codebook.shape
    count = len(places)
    first = places[0]
    rows = [cells] + [2 * edge, cells - 2 * edge] * (count - 1)
    return pl.pallas_call(
        functools.partial(lookup_body, count, edge),
        grid_spec=pltpu.PrefetchScalarGridSpec(
            num_scalar_prefetch=1,
            grid=(count, split),
            in_specs=[
                pl.BlockSpec((cells, codes // split), lambda i, j, order: (order[first + i], j)),
                pl.BlockSpec((codes // split, inner), lambda i, j, order: (j, 0)),
            ],
            out_specs=[pl.BlockSpec((height, inner), lambda i, j, order: (0, 0)) for height in rows],
            scratch_shapes=[pltpu.VMEM((cells, inner), WIDE)],
        ),
        out_shape=[jax.ShapeDtypeStruct((height, inner), NARROW) for height in rows],
        compiler_params=pltpu.CompilerParams(vmem_limit_bytes=WHOLE),
        cost_estimate=pl.CostEstimate(
            flops=2 * count * cells * codebook.size // COST, bytes_accessed=1, transcendentals=0
        ),
    )(info, weights, codebook)


def upstream_body(breadth, own, low, high, kernel, out, padded):
    edge = low.shape[0]
    cells = own.shape[0]
    tall = out.shape[0]
    padded[:edge] = low[...]
    padded[edge : edge + cells] = own[...]
    padded[edge + cells :] = high[...]
    for b in (1, 0, 2):
        total = sum(
            matmul_turned(padded[(2 - a) * breadth : (2 - a) * breadth + tall], kernel[a, b])
            for a in range(3)
        )
        total = step_columns(total, 1 - b, breadth)
        out[...] = total if b == 1 else out[...] + total


def upstream_back(own, low, high, kernel, breadth):
    cells, width = own.shape
    return call(
        functools.partial(upstream_body, breadth),
        (own, low, high, kernel),
        [((cells + 2 * breadth, kernel.shape[2]), WIDE)],
        2 * cells * kernel.size,
        [pltpu.VMEM((cells + 2 * low.shape[0], width), NARROW)],
    )[0]


def head_body(
    breadth, info, low, top, inner, bottom, high, kernel, grad_hidden, hidden, own_pre, field, grad, padded, grad_pre
):
    cells = grad.shape[0]
    tall = hidden.shape[0]
    at = 0
    for part in (low, top, inner, bottom, high):
        padded[at : at + part.shape[0]] = part[...]
        at += part.shape[0]
    field[...] = padded[breadth : breadth + tall]
    pre = sum(
        step_columns(
            sum(matmul(padded[a * breadth : a * breadth + tall], kernel[a, b]) for a in range(3)),
            b - 1,
            breadth,
        )
        for b in (1, 0, 2)
    )
    row = lax.broadcasted_iota(jnp.int32, pre.shape, 0)
    inside = ((row >= breadth) | (info[7] > 0)) & ((row < tall - breadth) | (info[8] > 0))
    sigma = 1.0 / (1.0 + jnp.exp(-pre))
    hidden[...] = jnp.where(inside, pre * sigma, 0.0).astype(NARROW)
    slope = grad_hidden[...] * (sigma * (1.0 + pre * (1.0 - sigma)))
    grad_pre[...] = jnp.where(inside, slope, 0.0).astype(NARROW)
    own_pre[...] = grad_pre[breadth : breadth + cells]
    total = sum(
        step_columns(
            sum(
                matmul_turned(
                    grad_pre[(2 - a) * breadth : (2 - a) * breadth + cells], kernel[a, b]
                )
                for a in range(3)
            ),
            1 - b,
            breadth,
        )
        for b in (1, 0, 2)
    )
    grad[...] = total.astype(NARROW)


def head(info, parts, kernel, grad_hidden, breadth):
    inputs = parts[0].shape[1]
    tall, width = grad_hidden.shape
    cells = tall - 2 * breadth
    return call(
        functools.partial(head_body, breadth),
        (info, *parts, kernel, grad_hidden),
        [((tall, width), NARROW), ((cells, width), NARROW), ((tall, inputs), NARROW), ((cells, inputs), NARROW)],
        4 * cells * kernel.size,
        [pltpu.VMEM((tall + 2 * breadth, inputs), NARROW), pltpu.VMEM((tall, width), NARROW)],
        spaces=(pltpu.SMEM,) + (pltpu.VMEM,) * 7,
    )


def decode_body(breadth, hidden, kernel, out):
    cells = out.shape[0]
    total = sum(
        step_columns(
            sum(matmul(hidden[a * breadth : a * breadth + cells], kernel[a, b]) for a in range(3)),
            b - 1,
            breadth,
        )
        for b in (1, 0, 2)
    )
    out[...] = total.astype(NARROW)


def decode(hidden, kernel, breadth):
    tall = hidden.shape[0]
    return call(
        functools.partial(decode_body, breadth),
        (hidden, kernel),
        [((tall - 2 * breadth, kernel.shape[3]), NARROW)],
        2 * (tall - 2 * breadth) * kernel.size,
    )[0]


def term_of(info, place, weights, field):
    cells = field.shape[0]
    rows = pl.ds(pl.multiple_of(info[place] * cells, cells), cells)
    return lax.dot_general(
        weights[rows, :], field[...], (((0,), (0,)), ((), ())), preferred_element_type=WIDE
    )


def book_start_body(info, weights, own, beside, across, out):
    out[...] = term_of(info, 3, weights, own)
    out[...] += term_of(info, 2, weights, beside)
    out[...] += term_of(info, 1, weights, across)


def book_end_body(info, weights, corner, base, mine, other, total):
    total[...] = base[...] + term_of(info, 0, weights, corner)
    half = mine.shape[0]
    core = info[9]
    mine[...] = total[pl.ds(pl.multiple_of(core * half, half), half), :].astype(NARROW)
    other[...] = total[pl.ds(pl.multiple_of((1 - core) * half, half), half), :].astype(NARROW)


def book_start(info, weights, own, beside, across):
    shape = (weights.shape[1], own.shape[1])
    return call(
        book_start_body,
        (info, weights, own, beside, across),
        [(shape, WIDE)],
        6 * weights.shape[1] * own.size,
        spaces=(pltpu.SMEM,) + (pltpu.VMEM,) * 4,
    )[0]


def book_end(info, weights, corner, base):
    half = (base.shape[0] // 2, base.shape[1])
    return (
        book_end_body,
        (info, weights, corner, base),
        [(half, NARROW), (half, NARROW)],
        [pltpu.VMEM(base.shape, WIDE)],
    )


def halves_body(mine, got, first, second):
    half = first.shape[0]
    first[...] = plus(mine[:half], got[:half])
    second[...] = plus(mine[half:], got[half:])


def halves(mine, got):
    half = (mine.shape[0] // 2, mine.shape[1])
    return halves_body, (mine, got), [(half, NARROW), (half, NARROW)], []


def pair_body(first, got_first, second, got_second, *outs):
    half = first.shape[0]
    if len(outs) == 2:
        outs[0][...] = plus(first[...], got_first[...])
        outs[1][...] = plus(second[...], got_second[...])
    else:
        outs[0][:half] = plus(first[...], got_first[...])
        outs[0][half:] = plus(second[...], got_second[...])


def pair(first, got_first, second, got_second, joined):
    rows, lanes = first.shape
    outs = [((2 * rows, lanes), NARROW)] if joined else [((rows, lanes), NARROW)] * 2
    return pair_body, (first, got_first, second, got_second), outs, []


def lay_out(breadth, pick, up, turned):
    half, cells = pick.shape[0], up.shape[0]
    across = matmul_turned(pick[...], up[...])
    column = lax.broadcasted_iota(jnp.int32, across.shape, 1) % breadth
    later = jnp.where(column == breadth - 1, 0.0, pltpu.roll(across, cells - 1, 1))
    sooner = jnp.where(column == 0, 0.0, pltpu.roll(across, 1, 1))
    for b, value in enumerate((later, across, sooner)):
        turned[b * half : (b + 1) * half, :] = value.astype(NARROW)


def own_grads_body(breadth, pick, up, pre, hidden, field, out, turned):
    width, cells = hidden.shape[1], up.shape[0]
    lay_out(breadth, pick, up, turned.at[0])
    lay_out(breadth, pick, pre, turned.at[1])

    @pl.loop(0, 3)
    def _(a):
        rows = pl.ds(pl.multiple_of(a * breadth, breadth), cells)
        out[a, :, :width] = matmul(turned[0], hidden[rows, :])
        out[a, :, width:] = matmul(turned[1], field[rows, :])


def far_grads_body(
    breadth, pick, up, pre, hidden, field, base, keep_a, send_a, keep_b, send_b, turned
):
    width, cells = hidden.shape[1], up.shape[0]
    half = pick.shape[0]
    parts = send_a.shape[0] + 1
    tall = half // parts
    short = tall // 2
    lay_out(breadth, pick, up, turned.at[0])
    lay_out(breadth, pick, pre, turned.at[1])

    @pl.loop(0, 3)
    def _(a):
        rows = pl.ds(pl.multiple_of(a * breadth, breadth), cells)
        for which, (array, start) in enumerate(((hidden, 0), (field, width))):
            inputs = array.shape[1]
            lanes = inputs // 2
            at = start // 2
            total = base[a, :, start : start + inputs] + matmul(turned[which], array[rows, :])
            total = total.astype(NARROW)
            for b in range(3):
                for k in range(parts):
                    block = total[b * half + k * tall : b * half + (k + 1) * tall]
                    if k == 0:
                        keep_a[a, b, :, at : at + lanes] = block[:, :lanes]
                    else:
                        send_a[k - 1, a, b, :, at : at + lanes] = block[:, :lanes]
                    keep_b[a, b, k, :, at : at + lanes] = block[:short, lanes:]
                    send_b[a, b, k, :, at : at + lanes] = block[short:, lanes:]


def kernel_grads(pick, own, far, breadth, parts):
    half, cells = pick.shape[0], own[0].shape[0]
    tall = half // parts
    inputs = own[2].shape[1] + own[3].shape[1]
    scratch = [pltpu.VMEM((2, 3 * half, cells), NARROW)]
    (base,) = call(
        functools.partial(own_grads_body, breadth),
        (pick, *own),
        [((3, 3 * half, inputs), WIDE)],
        18 * half * cells * inputs,
        scratch,
    )
    shapes = [
        (3, 3, tall, inputs // 2),
        (parts - 1, 3, 3, tall, inputs // 2),
        (3, 3, parts, tall // 2, inputs // 2),
        (3, 3, parts, tall // 2, inputs // 2),
    ]
    return call(
        functools.partial(far_grads_body, breadth),
        (pick, *far, base),
        [(shape, NARROW) for shape in shapes],
        18 * half * cells * inputs,
        scratch,
    )


def own_channels(width):
    parts = lax.axis_size("space") // 2
    space = lax.axis_index("space")
    code = lax.axis_index("code")
    clip = lax.axis_index("clip")
    grain = width // (parts * 16)
    index = jnp.arange(width // 2)
    inner = index % grain
    d_code = (index // grain) % 4
    d_clip = (index // (grain * 4)) % 2
    d_space = index // (grain * 8)
    owner = ((space ^ (2 * d_space)) * 4 + (code ^ d_code)) * 2 + (clip ^ d_clip)
    channel = owner * grain + inner
    return (channel[:, None] == jnp.arange(width)[None, :]).astype(NARROW)


def turn_body(keep_a, keep_b, got_b, *refs):
    keep_first, send_first, keep_second, send_second = refs[-4:]
    got_a = refs[:-4]
    short = keep_first.shape[2]
    for a in range(3):
        for b in range(3):
            total = plus(keep_a[a, b], *[got[a, b] for got in got_a])
            keep_first[a, b] = total[:short]
            send_first[a, b] = total[short:]
            total = plus(keep_b[a, b], got_b[a, b])
            keep_second[a, b] = total[0]
            for k in range(1, total.shape[0]):
                send_second[k - 1, a, b] = total[k]


def along_body(keep_first, got_first, keep_second, *refs):
    outs = refs[-4:] if refs[-1].shape[2] * 4 == keep_first.shape[2] else refs[-1:]
    got_second = refs[: -len(outs)]
    lanes = keep_first.shape[3]
    grain = keep_first.shape[2] // len(outs)
    for a in range(3):
        for b in range(3):
            first = plus(keep_first[a, b], got_first[a, b])
            second = plus(keep_second[a, b], *[got[a, b] for got in got_second])
            for k, out in enumerate(outs):
                out[a, b, :, :lanes] = first[k * grain : (k + 1) * grain]
                out[a, b, :, lanes:] = second[k * grain : (k + 1) * grain]


class Spread:
    def __init__(self, parts_of, name):
        self.keep_a, send_a, self.keep_b, send_b = parts_of
        self.name = name
        self.parts = send_a.shape[0] + 1
        self.got_a = [swap(send_a[k - 1], "space", 2 * k, name + "_a1") for k in range(1, self.parts)]
        self.got_b = swap(send_b, "clip", 1, name + "_b1")

    def turn(self):
        tall, lanes = self.keep_a.shape[2:]
        shape = (3, 3, tall // 2, lanes)
        outs = [(shape, NARROW)] * 3 + [((self.parts - 1,) + shape, NARROW)]
        return turn_body, (self.keep_a, self.keep_b, self.got_b, *self.got_a), outs, []

    def turned(self, outs):
        self.first, send_first, self.second, send_second = outs
        self.got_a = swap(send_first, "clip", 1, self.name + "_a2")
        self.got_b = [
            swap(send_second[k - 1], "space", 2 * k, self.name + "_b2") for k in range(1, self.parts)
        ]

    def along(self):
        rows, lanes = self.first.shape[2:]
        outs = [((3, 3, rows, 2 * lanes), NARROW)]
        if rows % 64 == 0:
            outs = [((3, 3, rows // 4, 2 * lanes), NARROW)] * 4
        return along_body, (self.first, self.got_a, self.second, *self.got_b), outs, []

    def sent(self, outs):
        if len(outs) == 1:
            grain = outs[0].shape[2] // 4
            outs = [outs[0][:, :, k * grain : (k + 1) * grain] for k in range(4)]
        self.last = outs[0]
        self.got = [swap(outs[k], "code", k, self.name + "_z") for k in (2, 1, 3)]

    def done(self, split):
        total = sum(got.astype(WIDE) for got in self.got) + self.last.astype(WIDE)
        total = total.transpose(0, 1, 3, 2)
        half = total.shape[2] // 2
        one = jnp.concatenate([total[:, :, split:half], total[:, :, half + split :]], axis=2)
        two = jnp.concatenate([total[:, :, :split], total[:, :, half : half + split]], axis=2)
        return one, two


def on_device(soft_weights, codebook, kernel_one, kernel_two, cotangent):
    weights = soft_weights[0]
    weights = weights.reshape(-1, weights.shape[2])
    own_rows, breadth, width = cotangent.shape[1:]
    upstream = cotangent[0]
    cells = own_rows * breadth
    own_up = upstream.reshape(cells, width)
    parts = lax.axis_size("space") // 2
    code = lax.axis_index("code")
    space = lax.axis_index("space")
    place = space * 4 + code
    last = lax.axis_size("space") * 4 - 1
    flat = lambda field: field.reshape(-1, field.shape[2])
    info = jnp.stack(
        [code ^ 3, code ^ 2, code ^ 1, code, code ^ 1, code ^ 2, code, place, last - place, space % 2]
    )
    info = info.astype(jnp.int32)

    edge = 2 * breadth
    (third,) = lookup((0,), info, weights, codebook, cells, edge, 2)
    from_pair = swap(third, "code", 1, "look_z1")
    shards = lookup((4, 5, 6), info, weights, after(codebook, third), cells, edge, 1)
    pick = after(own_channels(width), shards[0])
    (beside, second_ends, second, own_ends, own), pick = lax.optimization_barrier(
        (shards, pick)
    )
    middle_ends = plus(second_ends, from_pair[: 2 * edge])
    far_ends = swap(middle_ends, "code", 2, "look_ends")
    near = swap(beside, "code", 1, "look_near")
    middle = plus(after(second, middle_ends), from_pair[2 * edge :])
    far = swap(middle, "code", 2, "look_z2")
    upstream = after(own_up, middle)
    cot_low, cot_high = edges(upstream[:edge], upstream[-edge:], "cot_edge")
    part = lambda k: slice(k * edge, (k + 1) * edge)
    top, bottom = [
        plus(own_ends[part(k)], near[part(k)], far_ends[part(k)]) for k in range(2)
    ]
    low, high = edges(top, bottom, "embed_edge")
    upstream = after(own_up, top, bottom)
    far_up = swap(after(own_up, top), "space", 1, "cot_core")
    grad_hidden = upstream_back(upstream, cot_low, cot_high, kernel_two, breadth)
    inner = plus(after(own, top, bottom), near[2 * edge :], far)
    hidden, own_pre, field, grad_embedded = head(
        info, (low, top, inner, bottom, high), kernel_one, grad_hidden, breadth
    )

    across = swap(grad_embedded, "code", 2, "ge_z2")
    beside = swap(grad_embedded, "code", 1, "ge_z1")
    far_hidden = swap(hidden, "space", 1, "hidden_core")
    far_pre = swap(own_pre, "space", 1, "pre_core")
    far_field = swap(field, "space", 1, "field_core")
    grads = kernel_grads(
        pick,
        (own_up, own_pre, hidden, field),
        (far_up, far_pre, far_hidden, far_field),
        breadth,
        parts,
    )
    across, beside = after((across, beside), grads[0])
    grads = Spread(grads, "grads")
    corner = swap(across, "code", 1, "ge_z3")
    term = book_start(info, weights, grad_embedded, beside, across)
    (outs,) = fuse(grads.turn())
    grads.turned(outs)
    ((mine, other),) = fuse(book_end(info, weights, corner, after(term, grads.first)))
    got = swap(other, "space", 1, "book_core")
    ((first, second),) = fuse(halves(mine, got))

    stages = []
    bits = 2
    while bits < lax.axis_size("space"):
        stages.append(("space", bits))
        bits *= 2
    ways = list(zip(stages + [("clip", 1)], [("clip", 1)] + stages))
    for k, (way, back) in enumerate(ways):
        got_first, got_second = swap(first, *way, "book_a"), swap(second, *back, "book_b")
        if k == 0:
            decoded = decode(after(hidden, first), kernel_two, breadth)
            grads.second = after(grads.second, decoded)
            (outs,) = fuse(grads.along())
            grads.sent(outs)
            first = after(first, grads.last)
        (outs,) = fuse(pair(first, got_first, second, got_second, k == len(ways) - 1))
        if k < len(ways) - 1:
            first, second = outs
    (mine,) = outs
    other = swap(mine, "space", 1, "book_back")
    core = space % 2
    low = jnp.where(core == 0, mine, other)
    high = jnp.where(core == 0, other, mine)
    grad_codebook = jnp.concatenate([low, high], axis=0).astype(WIDE)
    grad_one, grad_two = grads.done(width // 2)
    return (decoded.reshape(cotangent.shape), grad_one, grad_two, grad_codebook)


def solution(mesh):
    in_specs = (
        P("clip", "space", None, "code"),
        P("code", None),
        P(),
        P(),
        P("clip", ("space", "code"), None, None),
    )
    out_specs = (
        P("clip", ("space", "code"), None, None),
        P(None, None, None, ("space", "code", "clip")),
        P(None, None, None, ("space", "code", "clip")),
        P("code", None),
    )
    return jax.shard_map(
        on_device, mesh=mesh, in_specs=in_specs, out_specs=out_specs, check_vma=False
    )
```

```python
import functools

import jax
import jax.numpy as jnp
from jax import lax
from jax.experimental import pallas as pl
from jax.experimental.pallas import tpu as pltpu
from jax.sharding import PartitionSpec as P

NARROW = jnp.bfloat16
WIDE = jnp.float32
COST = 8
SMALL, LARGE, WHOLE = 16 * 1024 * 1024, 24 * 1024 * 1024, 56 * 1024 * 1024


def swap(value, axis, bits, name):
    with jax.named_scope(name):
        return lax.ppermute(value, axis, [(i, i ^ bits) for i in range(lax.axis_size(axis))])


def after(value, *others):
    return lax.optimization_barrier((value, *others))[0]


def plus(*terms):
    return sum(term.astype(WIDE) for term in terms).astype(NARROW)


def edges(top, bottom, name):
    axes = ("space", "code")
    count = lax.axis_size(axes)
    forward = [(i, i + 1) for i in range(count - 1)]
    backward = [(i + 1, i) for i in range(count - 1)]
    with jax.named_scope(name):
        low = lax.ppermute(bottom, axes, forward)
        high = lax.ppermute(top, axes, backward)
    return low, high


def matmul(left, right):
    return jnp.dot(left, right, preferred_element_type=WIDE)


def matmul_turned(left, right):
    return lax.dot_general(left, right, (((1,), (1,)), ((), ())), preferred_element_type=WIDE)


def step_columns(value, offset, breadth):
    if offset == 0:
        return value
    count = value.shape[0]
    column = lax.broadcasted_iota(jnp.int32, value.shape, 0) % breadth
    moved = pltpu.roll(value, (-offset) % count, 0)
    return jnp.where(column == (0 if offset < 0 else breadth - 1), 0.0, moved)


def call(body, operands, outs, flops, scratch=(), limit=SMALL, spaces=None):
    local = pl.BlockSpec(memory_space=pltpu.VMEM)
    return pl.pallas_call(
        body,
        in_specs=[pl.BlockSpec(memory_space=space) for space in spaces] if spaces else [local] * len(operands),
        out_specs=[local] * len(outs),
        out_shape=[jax.ShapeDtypeStruct(shape, dtype) for shape, dtype in outs],
        scratch_shapes=list(scratch),
        compiler_params=pltpu.CompilerParams(vmem_limit_bytes=limit),
        cost_estimate=pl.CostEstimate(flops=flops // COST, bytes_accessed=1, transcendentals=0),
    )(*operands)


def fuse(*tasks):
    spans = [(len(operands), len(outs), len(scratch)) for _, operands, outs, scratch in tasks]
    counts = [sum(span[k] for span in spans) for k in range(3)]

    def body(*refs):
        at = [0, counts[0], counts[0] + counts[1]]
        for (task, *_), span in zip(tasks, spans):
            picked = []
            for k in range(3):
                picked += refs[at[k] : at[k] + span[k]]
                at[k] += span[k]
            task(*picked)

    operands = [operand for task in tasks for operand in task[1]]
    results = list(
        call(
            body,
            operands,
            [out for task in tasks for out in task[2]],
            8 * 10**8,
            [item for task in tasks for item in task[3]],
            spaces=[pltpu.SMEM if item.dtype == jnp.int32 else pltpu.VMEM for item in operands],
        )
    )
    return [[results.pop(0) for _ in range(span[1])] for span in spans]


def lookup_body(count, edge, order, weights, codebook, *refs):
    outs, total = refs[:-1], refs[-1]
    shard, step = pl.program_id(0), pl.program_id(1)
    last = pl.num_programs(1) - 1
    term = matmul(weights[...], codebook[...])

    @pl.when(step == 0)
    def _():
        total[...] = term

    @pl.when(step > 0)
    def _():
        total[...] += term

    for k in range(count):

        @pl.when((step == last) & (shard == k))
        def _():
            if len(outs) == count:
                ends, inner = outs[k].at[: 2 * edge], outs[k].at[2 * edge :]
            elif k == 0:
                ends, inner = outs[0].at[: 2 * edge], outs[0].at[2 * edge :]
            else:
                ends, inner = outs[2 * k - 1], outs[2 * k]
            ends[:edge] = total[:edge].astype(NARROW)
            ends[edge:] = total[-edge:].astype(NARROW)
            inner[...] = total[edge:-edge].astype(NARROW)


def lookup(places, info, weights, codebook, cells, edge, split):
    codes, inner = codebook.shape
    count = len(places)
    first = places[0]
    rows = [cells] + [2 * edge, cells - 2 * edge] * (count - 1)
    return pl.pallas_call(
        functools.partial(lookup_body, count, edge),
        grid_spec=pltpu.PrefetchScalarGridSpec(
            num_scalar_prefetch=1,
            grid=(count, split),
            in_specs=[
                pl.BlockSpec((cells, codes // split), lambda i, j, order: (order[first + i], j)),
                pl.BlockSpec((codes // split, inner), lambda i, j, order: (j, 0)),
            ],
            out_specs=[pl.BlockSpec((height, inner), lambda i, j, order: (0, 0)) for height in rows],
            scratch_shapes=[pltpu.VMEM((cells, inner), WIDE)],
        ),
        out_shape=[jax.ShapeDtypeStruct((height, inner), NARROW) for height in rows],
        compiler_params=pltpu.CompilerParams(vmem_limit_bytes=WHOLE),
        cost_estimate=pl.CostEstimate(
            flops=2 * count * cells * codebook.size // COST, bytes_accessed=1, transcendentals=0
        ),
    )(info, weights, codebook)


def upstream_body(breadth, own, low, high, kernel, out, padded):
    edge = low.shape[0]
    cells = own.shape[0]
    tall = out.shape[0]
    padded[:edge] = low[...]
    padded[edge : edge + cells] = own[...]
    padded[edge + cells :] = high[...]
    for b in (1, 0, 2):
        total = sum(
            matmul_turned(padded[(2 - a) * breadth : (2 - a) * breadth + tall], kernel[a, b])
            for a in range(3)
        )
        total = step_columns(total, 1 - b, breadth)
        out[...] = total if b == 1 else out[...] + total


def upstream_back(own, low, high, kernel, breadth):
    cells, width = own.shape
    return call(
        functools.partial(upstream_body, breadth),
        (own, low, high, kernel),
        [((cells + 2 * breadth, kernel.shape[2]), WIDE)],
        2 * cells * kernel.size,
        [pltpu.VMEM((cells + 2 * low.shape[0], width), NARROW)],
    )[0]


def head_body(
    breadth, info, low, top, inner, bottom, high, kernel, grad_hidden, hidden, own_pre, field, grad_pre, padded
):
    cells = own_pre.shape[0]
    tall = hidden.shape[0]
    at = 0
    for part in (low, top, inner, bottom, high):
        padded[at : at + part.shape[0]] = part[...]
        at += part.shape[0]
    field[...] = padded[breadth : breadth + tall]
    pre = sum(
        step_columns(
            sum(matmul(padded[a * breadth : a * breadth + tall], kernel[a, b]) for a in range(3)),
            b - 1,
            breadth,
        )
        for b in (1, 0, 2)
    )
    row = lax.broadcasted_iota(jnp.int32, pre.shape, 0)
    inside = ((row >= breadth) | (info[7] > 0)) & ((row < tall - breadth) | (info[8] > 0))
    sigma = 1.0 / (1.0 + jnp.exp(-pre))
    hidden[...] = jnp.where(inside, pre * sigma, 0.0).astype(NARROW)
    slope = grad_hidden[...] * (sigma * (1.0 + pre * (1.0 - sigma)))
    grad_pre[...] = jnp.where(inside, slope, 0.0).astype(NARROW)
    own_pre[...] = grad_pre[breadth : breadth + cells]


def embedded_body(breadth, grad_pre, kernel, grad):
    cells = grad.shape[0]
    total = sum(
        step_columns(
            sum(
                matmul_turned(
                    grad_pre[(2 - a) * breadth : (2 - a) * breadth + cells], kernel[a, b]
                )
                for a in range(3)
            ),
            1 - b,
            breadth,
        )
        for b in (1, 0, 2)
    )
    grad[...] = total.astype(NARROW)


def embedded_grad(grad_pre, kernel, breadth):
    cells = grad_pre.shape[0] - 2 * breadth
    return call(
        functools.partial(embedded_body, breadth),
        (grad_pre, kernel),
        [((cells, kernel.shape[2]), NARROW)],
        2 * cells * kernel.size,
    )[0]


def head(info, parts, kernel, grad_hidden, breadth):
    inputs = parts[0].shape[1]
    tall, width = grad_hidden.shape
    cells = tall - 2 * breadth
    return call(
        functools.partial(head_body, breadth),
        (info, *parts, kernel, grad_hidden),
        [((tall, width), NARROW), ((cells, width), NARROW), ((tall, inputs), NARROW), ((tall, width), NARROW)],
        4 * cells * kernel.size,
        [pltpu.VMEM((tall + 2 * breadth, inputs), NARROW)],
        spaces=(pltpu.SMEM,) + (pltpu.VMEM,) * 7,
    )


def decode_body(breadth, hidden, kernel, out):
    cells = out.shape[0]
    total = sum(
        step_columns(
            sum(matmul(hidden[a * breadth : a * breadth + cells], kernel[a, b]) for a in range(3)),
            b - 1,
            breadth,
        )
        for b in (1, 0, 2)
    )
    out[...] = total.astype(NARROW)


def decode(hidden, kernel, breadth):
    tall = hidden.shape[0]
    return call(
        functools.partial(decode_body, breadth),
        (hidden, kernel),
        [((tall - 2 * breadth, kernel.shape[3]), NARROW)],
        2 * (tall - 2 * breadth) * kernel.size,
    )[0]


def term_of(info, place, weights, field):
    cells = field.shape[0]
    rows = pl.ds(pl.multiple_of(info[place] * cells, cells), cells)
    return lax.dot_general(
        weights[rows, :], field[...], (((0,), (0,)), ((), ())), preferred_element_type=WIDE
    )


def book_start_body(info, weights, own, beside, across, out):
    out[...] = term_of(info, 3, weights, own)
    out[...] += term_of(info, 2, weights, beside)
    out[...] += term_of(info, 1, weights, across)


def book_end_body(info, weights, corner, base, mine, other, total):
    total[...] = base[...] + term_of(info, 0, weights, corner)
    half = mine.shape[0]
    core = info[9]
    mine[...] = total[pl.ds(pl.multiple_of(core * half, half), half), :].astype(NARROW)
    other[...] = total[pl.ds(pl.multiple_of((1 - core) * half, half), half), :].astype(NARROW)


def book_start(info, weights, own, beside, across):
    shape = (weights.shape[1], own.shape[1])
    return call(
        book_start_body,
        (info, weights, own, beside, across),
        [(shape, WIDE)],
        6 * weights.shape[1] * own.size,
        spaces=(pltpu.SMEM,) + (pltpu.VMEM,) * 4,
    )[0]


def book_end(info, weights, corner, base):
    half = (base.shape[0] // 2, base.shape[1])
    return (
        book_end_body,
        (info, weights, corner, base),
        [(half, NARROW), (half, NARROW)],
        [pltpu.VMEM(base.shape, WIDE)],
    )


def halves_body(mine, got, first, second):
    half = first.shape[0]
    first[...] = plus(mine[:half], got[:half])
    second[...] = plus(mine[half:], got[half:])


def halves(mine, got):
    half = (mine.shape[0] // 2, mine.shape[1])
    return halves_body, (mine, got), [(half, NARROW), (half, NARROW)], []


def pair_body(first, got_first, second, got_second, *outs):
    half = first.shape[0]
    if len(outs) == 2:
        outs[0][...] = plus(first[...], got_first[...])
        outs[1][...] = plus(second[...], got_second[...])
    else:
        outs[0][:half] = plus(first[...], got_first[...])
        outs[0][half:] = plus(second[...], got_second[...])


def pair(first, got_first, second, got_second, joined):
    rows, lanes = first.shape
    outs = [((2 * rows, lanes), NARROW)] if joined else [((rows, lanes), NARROW)] * 2
    return pair_body, (first, got_first, second, got_second), outs, []


def lay_out(breadth, pick, up, turned):
    half, cells = pick.shape[0], up.shape[0]
    across = matmul_turned(pick[...], up[...])
    column = lax.broadcasted_iota(jnp.int32, across.shape, 1) % breadth
    later = jnp.where(column == breadth - 1, 0.0, pltpu.roll(across, cells - 1, 1))
    sooner = jnp.where(column == 0, 0.0, pltpu.roll(across, 1, 1))
    for b, value in enumerate((later, across, sooner)):
        turned[b * half : (b + 1) * half, :] = value.astype(NARROW)


def own_grads_body(breadth, pick, up, pre, hidden, field, out, turned):
    width, cells = hidden.shape[1], up.shape[0]
    lay_out(breadth, pick, up, turned.at[0])
    lay_out(breadth, pick, pre, turned.at[1])

    @pl.loop(0, 3)
    def _(a):
        rows = pl.ds(pl.multiple_of(a * breadth, breadth), cells)
        out[a, :, :width] = matmul(turned[0], hidden[rows, :])
        out[a, :, width:] = matmul(turned[1], field[rows, :])


def far_grads_body(
    breadth, pick, up, pre, hidden, field, base, keep_a, send_a, keep_b, send_b, turned
):
    width, cells = hidden.shape[1], up.shape[0]
    half = pick.shape[0]
    parts = send_a.shape[0] + 1
    tall = half // parts
    short = tall // 2
    lay_out(breadth, pick, up, turned.at[0])
    lay_out(breadth, pick, pre, turned.at[1])

    @pl.loop(0, 3)
    def _(a):
        rows = pl.ds(pl.multiple_of(a * breadth, breadth), cells)
        for which, (array, start) in enumerate(((hidden, 0), (field, width))):
            inputs = array.shape[1]
            lanes = inputs // 2
            at = start // 2
            total = base[a, :, start : start + inputs] + matmul(turned[which], array[rows, :])
            total = total.astype(NARROW)
            for b in range(3):
                for k in range(parts):
                    block = total[b * half + k * tall : b * half + (k + 1) * tall]
                    if k == 0:
                        keep_a[a, b, :, at : at + lanes] = block[:, :lanes]
                    else:
                        send_a[k - 1, a, b, :, at : at + lanes] = block[:, :lanes]
                    keep_b[a, b, k, :, at : at + lanes] = block[:short, lanes:]
                    send_b[a, b, k, :, at : at + lanes] = block[short:, lanes:]


def kernel_grads(pick, own, far, breadth, parts):
    half, cells = pick.shape[0], own[0].shape[0]
    tall = half // parts
    inputs = own[2].shape[1] + own[3].shape[1]
    scratch = [pltpu.VMEM((2, 3 * half, cells), NARROW)]
    (base,) = call(
        functools.partial(own_grads_body, breadth),
        (pick, *own),
        [((3, 3 * half, inputs), WIDE)],
        18 * half * cells * inputs,
        scratch,
    )
    shapes = [
        (3, 3, tall, inputs // 2),
        (parts - 1, 3, 3, tall, inputs // 2),
        (3, 3, parts, tall // 2, inputs // 2),
        (3, 3, parts, tall // 2, inputs // 2),
    ]
    return call(
        functools.partial(far_grads_body, breadth),
        (pick, *far, base),
        [(shape, NARROW) for shape in shapes],
        18 * half * cells * inputs,
        scratch,
    )


def own_channels(width):
    parts = lax.axis_size("space") // 2
    space = lax.axis_index("space")
    code = lax.axis_index("code")
    clip = lax.axis_index("clip")
    grain = width // (parts * 16)
    index = jnp.arange(width // 2)
    inner = index % grain
    d_code = (index // grain) % 4
    d_clip = (index // (grain * 4)) % 2
    d_space = index // (grain * 8)
    owner = ((space ^ (2 * d_space)) * 4 + (code ^ d_code)) * 2 + (clip ^ d_clip)
    channel = owner * grain + inner
    return (channel[:, None] == jnp.arange(width)[None, :]).astype(NARROW)


def turn_body(keep_a, keep_b, got_b, *refs):
    keep_first, send_first, keep_second, send_second = refs[-4:]
    got_a = refs[:-4]
    short = keep_first.shape[2]
    for a in range(3):
        for b in range(3):
            total = plus(keep_a[a, b], *[got[a, b] for got in got_a])
            keep_first[a, b] = total[:short]
            send_first[a, b] = total[short:]
            total = plus(keep_b[a, b], got_b[a, b])
            keep_second[a, b] = total[0]
            for k in range(1, total.shape[0]):
                send_second[k - 1, a, b] = total[k]


def along_body(keep_first, got_first, keep_second, *refs):
    outs = refs[-4:] if refs[-1].shape[2] * 4 == keep_first.shape[2] else refs[-1:]
    got_second = refs[: -len(outs)]
    lanes = keep_first.shape[3]
    grain = keep_first.shape[2] // len(outs)
    for a in range(3):
        for b in range(3):
            first = plus(keep_first[a, b], got_first[a, b])
            second = plus(keep_second[a, b], *[got[a, b] for got in got_second])
            for k, out in enumerate(outs):
                out[a, b, :, :lanes] = first[k * grain : (k + 1) * grain]
                out[a, b, :, lanes:] = second[k * grain : (k + 1) * grain]


class Spread:
    def __init__(self, parts_of, name):
        self.keep_a, send_a, self.keep_b, send_b = parts_of
        self.name = name
        self.parts = send_a.shape[0] + 1
        self.got_a = [swap(send_a[k - 1], "space", 2 * k, name + "_a1") for k in range(1, self.parts)]
        self.got_b = swap(send_b, "clip", 1, name + "_b1")

    def turn(self):
        tall, lanes = self.keep_a.shape[2:]
        shape = (3, 3, tall // 2, lanes)
        outs = [(shape, NARROW)] * 3 + [((self.parts - 1,) + shape, NARROW)]
        return turn_body, (self.keep_a, self.keep_b, self.got_b, *self.got_a), outs, []

    def turned(self, outs):
        self.first, send_first, self.second, send_second = outs
        self.got_a = swap(send_first, "clip", 1, self.name + "_a2")
        self.got_b = [
            swap(send_second[k - 1], "space", 2 * k, self.name + "_b2") for k in range(1, self.parts)
        ]

    def along(self):
        rows, lanes = self.first.shape[2:]
        outs = [((3, 3, rows, 2 * lanes), NARROW)]
        if rows % 64 == 0:
            outs = [((3, 3, rows // 4, 2 * lanes), NARROW)] * 4
        return along_body, (self.first, self.got_a, self.second, *self.got_b), outs, []

    def sent(self, outs):
        if len(outs) == 1:
            grain = outs[0].shape[2] // 4
            outs = [outs[0][:, :, k * grain : (k + 1) * grain] for k in range(4)]
        self.last = outs[0]
        self.got = [swap(outs[k], "code", k, self.name + "_z") for k in (2, 1, 3)]

    def done(self, split):
        total = sum(got.astype(WIDE) for got in self.got) + self.last.astype(WIDE)
        total = total.transpose(0, 1, 3, 2)
        half = total.shape[2] // 2
        one = jnp.concatenate([total[:, :, split:half], total[:, :, half + split :]], axis=2)
        two = jnp.concatenate([total[:, :, :split], total[:, :, half : half + split]], axis=2)
        return one, two


def on_device(soft_weights, codebook, kernel_one, kernel_two, cotangent):
    weights = soft_weights[0]
    weights = weights.reshape(-1, weights.shape[2])
    own_rows, breadth, width = cotangent.shape[1:]
    upstream = cotangent[0]
    cells = own_rows * breadth
    own_up = upstream.reshape(cells, width)
    parts = lax.axis_size("space") // 2
    code = lax.axis_index("code")
    space = lax.axis_index("space")
    place = space * 4 + code
    last = lax.axis_size("space") * 4 - 1
    flat = lambda field: field.reshape(-1, field.shape[2])
    info = jnp.stack(
        [code ^ 3, code ^ 2, code ^ 1, code, code ^ 1, code ^ 2, code, place, last - place, space % 2]
    )
    info = info.astype(jnp.int32)

    edge = 2 * breadth
    (third,) = lookup((0,), info, weights, codebook, cells, edge, 2)
    from_pair = swap(third, "code", 1, "look_z1")
    shards = lookup((4, 5, 6), info, weights, after(codebook, third), cells, edge, 1)
    pick = after(own_channels(width), shards[0])
    (beside, second_ends, second, own_ends, own), pick = lax.optimization_barrier(
        (shards, pick)
    )
    middle_ends = plus(second_ends, from_pair[: 2 * edge])
    far_ends = swap(middle_ends, "code", 2, "look_ends")
    near = swap(beside, "code", 1, "look_near")
    middle = plus(after(second, middle_ends), from_pair[2 * edge :])
    far = swap(middle, "code", 2, "look_z2")
    upstream = after(own_up, middle)
    cot_low, cot_high = edges(upstream[:edge], upstream[-edge:], "cot_edge")
    part = lambda k: slice(k * edge, (k + 1) * edge)
    top, bottom = [
        plus(own_ends[part(k)], near[part(k)], far_ends[part(k)]) for k in range(2)
    ]
    low, high = edges(top, bottom, "embed_edge")
    upstream = after(own_up, top, bottom)
    far_up = swap(after(own_up, top), "space", 1, "cot_core")
    grad_hidden = upstream_back(upstream, cot_low, cot_high, kernel_two, breadth)
    inner = plus(after(own, top, bottom), near[2 * edge :], far)
    hidden, own_pre, field, grad_pre = head(
        info, (low, top, inner, bottom, high), kernel_one, grad_hidden, breadth
    )

    far_hidden = swap(hidden, "space", 1, "hidden_core")
    far_pre = swap(own_pre, "space", 1, "pre_core")
    far_field = swap(field, "space", 1, "field_core")
    grads = kernel_grads(
        pick,
        (own_up, own_pre, hidden, field),
        (far_up, far_pre, far_hidden, far_field),
        breadth,
        parts,
    )
    grad_embedded = embedded_grad(after(grad_pre, grads[0]), kernel_one, breadth)
    across = swap(grad_embedded, "code", 2, "ge_z2")
    beside = swap(grad_embedded, "code", 1, "ge_z1")
    grads = Spread(grads, "grads")
    corner = swap(across, "code", 1, "ge_z3")
    term = book_start(info, weights, grad_embedded, beside, across)
    (outs,) = fuse(grads.turn())
    grads.turned(outs)
    ((mine, other),) = fuse(book_end(info, weights, corner, after(term, grads.first)))
    got = swap(other, "space", 1, "book_core")
    ((first, second),) = fuse(halves(mine, got))

    stages = []
    bits = 2
    while bits < lax.axis_size("space"):
        stages.append(("space", bits))
        bits *= 2
    ways = list(zip(stages + [("clip", 1)], [("clip", 1)] + stages))
    for k, (way, back) in enumerate(ways):
        got_first, got_second = swap(first, *way, "book_a"), swap(second, *back, "book_b")
        if k == 0:
            decoded = decode(after(hidden, first), kernel_two, breadth)
            grads.second = after(grads.second, decoded)
            (outs,) = fuse(grads.along())
            grads.sent(outs)
            first = after(first, grads.last)
        (outs,) = fuse(pair(first, got_first, second, got_second, k == len(ways) - 1))
        if k < len(ways) - 1:
            first, second = outs
    (mine,) = outs
    other = swap(mine, "space", 1, "book_back")
    core = space % 2
    low = jnp.where(core == 0, mine, other)
    high = jnp.where(core == 0, other, mine)
    grad_codebook = jnp.concatenate([low, high], axis=0).astype(WIDE)
    grad_one, grad_two = grads.done(width // 2)
    return (decoded.reshape(cotangent.shape), grad_one, grad_two, grad_codebook)


def solution(mesh):
    in_specs = (
        P("clip", "space", None, "code"),
        P("code", None),
        P(),
        P(),
        P("clip", ("space", "code"), None, None),
    )
    out_specs = (
        P("clip", ("space", "code"), None, None),
        P(None, None, None, ("space", "code", "clip")),
        P(None, None, None, ("space", "code", "clip")),
        P("code", None),
    )
    return jax.shard_map(
        on_device, mesh=mesh, in_specs=in_specs, out_specs=out_specs, check_vma=False
    )
```
